32 devices in a mesh: groups: 2 (over x), slab: 16 (over z, y, core).
Axes of the slice: x: 2, y: 2, z: 4, core: 2. Of those that a mesh axis runs over, the one named last changes fastest.
Arguments:
- melt_speeds: float32 [3, 64, 32, 512], P(None, ('groups', 'slab')), parts along dimension 1, may hold values from -3 to 3
- heat_state: float32 [64, 32, 512], P(('groups', 'slab')), parts along dimension 0, may hold values from -4 to 4
- eddy_quantities: float32 [2, 64, 32, 512], P(None, ('groups', 'slab')), parts along dimension 1, may hold values from 0.02 to 1
- zone_labels: int32 [32, 16, 256], P(('groups', 'slab')), parts along dimension 0, may hold values from 0 to 7
- zone_resistivity_inverse: float32 [8], replicated, may hold values from 0.05 to 0.4
- imposed_induction: float32 [3, 512, 16, 16], P(None, ('groups', 'slab')), parts along dimension 1, may hold values from -4 to 4
- winding_current: float32 [3, 512, 16, 16], P(None, ('groups', 'slab')), parts along dimension 1, may hold values from -4 to 4
- window_entry_induction_guess: float32 [3, 512, 16, 16], P(None, ('groups', 'slab')), parts along dimension 1, may hold values from 1 to 4
Outputs:
- velocity_out: float32 [3, 64, 32, 512], P(None, ('groups', 'slab')), parts along dimension 1
- temperature_out: float32 [64, 32, 512], P(('groups', 'slab')), parts along dimension 0
- turbulence_out: float32 [2, 64, 32, 512], P(None, ('groups', 'slab')), parts along dimension 1
- potential: float32 [3, 512, 16, 16], P(None, ('groups', 'slab')), parts along dimension 1
The draws below stay inside these ranges and needn't reach their ends.
There are 2 independent parts, one for each index of `groups`. The reference program is written for one: setup_inputs(seed, part) draws one part's arguments, and reference() takes and returns one part's arrays. A program takes and returns all parts, laid end to end along the dimension named above; an argument that names none is the same for every part. Nothing has to cross between parts.
Inputs may be any that keep to these rules, and one draw needn't show every extreme that they name: `zone_labels`: region number of each coarse block.
All inputs are finite; a program needn't handle non-finite values.
Results may differ from the reference program's by a relative error of at most 0.0001.
Values sent between devices are 32-bit elements; how exact they have to be, the bound alone decides.
A program may use at most 128 MiB of HBM per device.

```python
import math
import jax
import jax.numpy as jnp

NARROW_BINS_NORTH = 32
NARROW_BINS_EAST = 512
STEPS = 2
SWEEPS = 8
REGIONS = 8
NARROW_BINS_HIGH = 32
XH = 256
YH = 16
ZH = 16


def draw_window_entry_induction_guess(key, part):
    phase_key = jax.random.fold_in(key, 71)
    rough_key = jax.random.fold_in(key, 72)
    phase = jax.random.uniform(phase_key, (3, 1, 1, 1), jnp.float32, 0.0, 2.0 * math.pi)
    depth = jnp.arange(ZH, dtype=jnp.float32)[None, None, None, :]
    wave = jnp.cos(4.0 * math.pi * depth / ZH + phase)
    rough = jnp.clip(0.4 * jax.random.normal(rough_key, (3, XH, YH, ZH), jnp.float32), -0.8, 0.8)
    return (2.5 + 0.6 * wave + rough).astype(jnp.float32)


def set_ends(entries, rng, smallest, high):
    longest = entries.shape.index(max(entries.shape))
    spots = []
    for shift in (0, 1):
        where = [jax.random.randint(jax.random.fold_in(rng, axis), (), 0, length) for axis, length in enumerate(entries.shape)]
        where[longest] = (where[longest] + shift) % entries.shape[longest]
        spots.append(tuple(where))
    return entries.at[spots[0]].set(smallest).at[spots[1]].set(high)


def shard_levels(key, shape, shards, low, high):
    def one(dim, shards_of):
        heights = jax.random.uniform(jax.random.fold_in(jax.random.fold_in(key, 6), dim), (shards_of,), jnp.float32, low / len(shards), high / len(shards))
        return jnp.repeat(jnp.exp(heights), shape[dim] // shards_of).reshape((-1,) + (1,) * (len(shape) - dim - 1))

    level = one(*shards[0])
    for cut in shards[1:]:
        level = level * one(*cut)
    return level


def gaussian(key, dims, scale, limit, shards=(), kind=jnp.bfloat16):
    array = scale * jax.random.normal(key, dims, jnp.float32)
    if shards:
        array = array * shard_levels(key, dims, shards, -0.22, 0.18)
    return jnp.clip(array, -limit, limit).astype(kind)


def setup_inputs(seed: int = 0, part: int = 0) -> dict:
    seeds = jax.random.split(jax.random.key(seed), 9)
    part_splits = jax.random.split(jax.random.fold_in(seeds[8], part), 9)
    return {
        "melt_speeds": gaussian(part_splits[0], (3, NARROW_BINS_HIGH, NARROW_BINS_NORTH, NARROW_BINS_EAST), 0.5, 3.0, ((1, 16),), jnp.float32),
        "heat_state": gaussian(part_splits[1], (NARROW_BINS_HIGH, NARROW_BINS_NORTH, NARROW_BINS_EAST), 1.0, 4.0, ((0, 16),), jnp.float32),
        "eddy_quantities": jnp.clip(jnp.exp(math.log(1.0) - 3.912023 * jax.random.uniform(part_splits[2], (2, NARROW_BINS_HIGH, NARROW_BINS_NORTH, NARROW_BINS_EAST), jnp.float32) ** shard_levels(part_splits[2], (2, NARROW_BINS_HIGH, NARROW_BINS_NORTH, NARROW_BINS_EAST), ((1, 16),), -0.2, 0.2)), 0.02, 1.0),
        "zone_labels": set_ends(jax.random.randint(part_splits[3], (ZH, YH, XH), 0, REGIONS), jax.random.fold_in(part_splits[3], 1), 0, REGIONS - 1).astype(jnp.int32),
        "zone_resistivity_inverse": jnp.clip(jnp.exp(jax.random.uniform(seeds[4], (REGIONS,), jnp.float32, math.log(0.05), math.log(0.4))), 0.05, 0.4),
        "imposed_induction": gaussian(part_splits[5], (3, XH, YH, ZH), 1.0, 4.0, ((1, 16),), jnp.float32),
        "winding_current": gaussian(part_splits[6], (3, XH, YH, ZH), 1.0, 4.0, ((1, 16),), jnp.float32),
        "window_entry_induction_guess": draw_window_entry_induction_guess(jax.random.fold_in(jax.random.fold_in(seeds[8], part), 71), part),
    }


time_step = 0.02
molecular = 0.01
heat_diffuse = 0.01
eddy_coeff = 0.09
prod_coeff = 1.44
dissip_coeff = 1.92
turb_floor = 0.05
coupling = 1.0
thermal_gradient_factor = 0.3


def reduce_onto_parent(block):
    comps, depth, rows, cols = block.shape
    shaped = block.reshape(comps, depth // 2, 2, rows // 2, 2, cols // 2, 2)
    return jnp.mean(shaped, axis=(2, 4, 6))


def prolong(block):
    comps, depth, rows, cols = block.shape
    wide = jnp.broadcast_to(block[:, :, None, :, None, :, None], (comps, depth, 2, rows, 2, cols, 2))
    return wide.reshape(comps, depth * 2, rows * 2, cols * 2)


def cross(left_vec, right_vec):
    return jnp.stack([left_vec[1] * right_vec[2] - left_vec[2] * right_vec[1],
                      left_vec[2] * right_vec[0] - left_vec[0] * right_vec[2],
                      left_vec[0] * right_vec[1] - left_vec[1] * right_vec[0]], 0)


def neighbours(padded):
    return (padded[:, 2:, 1:-1, 1:-1] + padded[:, :-2, 1:-1, 1:-1] + padded[:, 1:-1, 2:, 1:-1]
            + padded[:, 1:-1, :-2, 1:-1] + padded[:, 1:-1, 1:-1, 2:] + padded[:, 1:-1, 1:-1, :-2])


def ohmic_admittance(zone_labels, zone_resistivity_inverse, heat_state):
    labels = jnp.arange(zone_resistivity_inverse.shape[0], dtype=jnp.int32)
    onehot = zone_labels[None] == labels[:, None, None, None]
    searched_higher = jnp.sum(jnp.where(onehot, zone_resistivity_inverse[:, None, None, None], jnp.float32(0.0)), axis=0)
    return searched_higher * reduce_onto_parent(jnp.exp(-thermal_gradient_factor * heat_state)[None])[0]


def relax(coupled, imposed_induction, winding_current, potential, face_fn):
    conduct = coupled[3]
    motional = cross(coupled[:3], imposed_induction)
    source = conduct * motional + winding_current
    diagonal = 6.0 + coupling * conduct
    for sweep_index in range(SWEEPS):
        potential = (source + neighbours(face_fn(potential))) / diagonal
    drive_field = motional - coupling * potential
    current = conduct * drive_field + winding_current
    lorentz = cross(current, imposed_induction)
    joule = conduct * jnp.sum(drive_field * drive_field, axis=0)
    return potential, jnp.concatenate([lorentz, joule[None]], 0)


def advance(padded, lorentz, joule):
    bordered = jnp.pad(padded, ((0, 0), (0, 0), (0, 0), (1, 1)))
    center = bordered[:, 1:-1, 1:-1, 1:-1]
    z_plus = bordered[:, 2:, 1:-1, 1:-1]
    z_minus = bordered[:, :-2, 1:-1, 1:-1]
    y_plus = bordered[:, 1:-1, 2:, 1:-1]
    y_minus = bordered[:, 1:-1, :-2, 1:-1]
    x_plus = bordered[:, 1:-1, 1:-1, 2:]
    x_minus = bordered[:, 1:-1, 1:-1, :-2]
    grad_z = 0.5 * (z_plus - z_minus)
    grad_y = 0.5 * (y_plus - y_minus)
    grad_x = 0.5 * (x_plus - x_minus)
    laplace = z_plus + z_minus + y_plus + y_minus + x_plus + x_minus - 6.0 * center
    kinetic = center[4]
    dissip = center[5]
    transport = center[0] * grad_x + center[1] * grad_y + center[2] * grad_z
    eddy_visc = eddy_coeff * kinetic * kinetic / jnp.maximum(dissip, turb_floor)
    strain = jnp.sum(grad_x[:3] * grad_x[:3] + grad_y[:3] * grad_y[:3] + grad_z[:3] * grad_z[:3], axis=0)
    produce = eddy_visc * strain
    diffuse = jnp.stack([molecular + eddy_visc, molecular + eddy_visc, molecular + eddy_visc,
                         heat_diffuse + eddy_visc / 0.9, molecular + eddy_visc, molecular + eddy_visc / 1.3], 0)
    dissip_source = (prod_coeff * produce - dissip_coeff * dissip) * dissip / jnp.maximum(kinetic, turb_floor)
    source = jnp.concatenate([lorentz, joule[None], (produce - dissip)[None], dissip_source[None]], 0)
    return center + time_step * (diffuse * laplace - transport + source)


def pad_all(potential):
    return jnp.pad(potential, ((0, 0), (1, 1), (1, 1), (1, 1)))


def reference(melt_speeds, heat_state, eddy_quantities, zone_labels, zone_resistivity_inverse, imposed_induction, winding_current, window_entry_induction_guess):
    induction_tables = jnp.concatenate([melt_speeds, heat_state[None], eddy_quantities], 0)
    potential = window_entry_induction_guess
    for step_index in range(STEPS):
        conduct = ohmic_admittance(zone_labels, zone_resistivity_inverse, induction_tables[3])
        coupled = jnp.concatenate([reduce_onto_parent(induction_tables[:3]), conduct[None]], 0)
        coupled = jnp.transpose(coupled, (0, 3, 2, 1))
        potential, em_loads = relax(coupled, imposed_induction, winding_current, potential, pad_all)
        em_loads = prolong(jnp.transpose(em_loads, (0, 3, 2, 1)))
        padded = jnp.pad(induction_tables, ((0, 0), (1, 1), (1, 1), (0, 0)))
        induction_tables = advance(padded, em_loads[:3], em_loads[3])
    return induction_tables[:3], induction_tables[3], induction_tables[4:], potential
```

```python
import functools

import jax
import jax.numpy as jnp
from jax import lax
from jax.experimental import pallas as pl
from jax.experimental.pallas import tpu as pltpu
from jax.sharding import PartitionSpec as P

STEPS = 2
SWEEPS = 8


time_step = 0.02
molecular = 0.01
heat_diffuse = 0.01
eddy_coeff = 0.09
prod_coeff = 1.44
dissip_coeff = 1.92
turb_floor = 0.05
coupling = 1.0
thermal_gradient_factor = 0.3


def extended(block, sides, width):
    for axis, dim in sides:
        count = lax.axis_size(axis)
        forward = [(i, i + 1) for i in range(count - 1)]
        backward = [(target, source) for source, target in forward]
        low = lax.ppermute(
            lax.slice_in_dim(block, block.shape[dim] - width, None, axis=dim), axis, forward
        )
        high = lax.ppermute(lax.slice_in_dim(block, 0, width, axis=dim), axis, backward)
        block = jnp.concatenate([low, block, high], axis=dim)
    return block


def reduce_onto_parent(block):
    comps, depth, rows, cols = block.shape
    shaped = block.reshape(comps, depth // 2, 2, rows // 2, 2, cols // 2, 2)
    return jnp.mean(shaped, axis=(2, 4, 6))


def prolong(block):
    comps, depth, rows, cols = block.shape
    wide = jnp.broadcast_to(
        block[:, :, None, :, None, :, None], (comps, depth, 2, rows, 2, cols, 2)
    )
    return wide.reshape(comps, depth * 2, rows * 2, cols * 2)


def cross(left_vec, right_vec):
    return jnp.stack(
        [
            left_vec[1] * right_vec[2] - left_vec[2] * right_vec[1],
            left_vec[2] * right_vec[0] - left_vec[0] * right_vec[2],
            left_vec[0] * right_vec[1] - left_vec[1] * right_vec[0],
        ],
        0,
    )


def neighbours(padded):
    return (
        padded[:, 2:, 1:-1, 1:-1]
        + padded[:, :-2, 1:-1, 1:-1]
        + padded[:, 1:-1, 2:, 1:-1]
        + padded[:, 1:-1, :-2, 1:-1]
        + padded[:, 1:-1, 1:-1, 2:]
        + padded[:, 1:-1, 1:-1, :-2]
    )


def ohmic_admittance(zone_labels, zone_resistivity_inverse, heat_state):
    labels = jnp.arange(zone_resistivity_inverse.shape[0], dtype=jnp.int32)
    onehot = zone_labels[None] == labels[:, None, None, None]
    searched_higher = jnp.sum(
        jnp.where(onehot, zone_resistivity_inverse[:, None, None, None], jnp.float32(0.0)), axis=0
    )
    return (
        searched_higher
        * reduce_onto_parent(jnp.exp(-thermal_gradient_factor * heat_state)[None])[0]
    )


def faces(potential):
    padded = extended(potential, (("slab", 1),), 1)
    return jnp.pad(padded, ((0, 0), (0, 0), (1, 1), (1, 1)))


def relax(coupled, imposed_induction, winding_current, potential):
    conduct = coupled[3]
    motional = cross(coupled[:3], imposed_induction)
    source = conduct * motional + winding_current
    diagonal = 6.0 + coupling * conduct
    for sweep_index in range(SWEEPS):
        potential = (source + neighbours(faces(potential))) / diagonal
    drive_field = motional - coupling * potential
    current = conduct * drive_field + winding_current
    lorentz = cross(current, imposed_induction)
    joule = conduct * jnp.sum(drive_field * drive_field, axis=0)
    return (potential, jnp.concatenate([lorentz, joule[None]], 0))


def advance(padded, lorentz, joule):
    bordered = jnp.pad(padded, ((0, 0), (0, 0), (0, 0), (1, 1)))
    center = bordered[:, 1:-1, 1:-1, 1:-1]
    z_plus = bordered[:, 2:, 1:-1, 1:-1]
    z_minus = bordered[:, :-2, 1:-1, 1:-1]
    y_plus = bordered[:, 1:-1, 2:, 1:-1]
    y_minus = bordered[:, 1:-1, :-2, 1:-1]
    x_plus = bordered[:, 1:-1, 1:-1, 2:]
    x_minus = bordered[:, 1:-1, 1:-1, :-2]
    grad_z = 0.5 * (z_plus - z_minus)
    grad_y = 0.5 * (y_plus - y_minus)
    grad_x = 0.5 * (x_plus - x_minus)
    laplace = z_plus + z_minus + y_plus + y_minus + x_plus + x_minus - 6.0 * center
    kinetic = center[4]
    dissip = center[5]
    transport = center[0] * grad_x + center[1] * grad_y + center[2] * grad_z
    eddy_visc = eddy_coeff * kinetic * kinetic / jnp.maximum(dissip, turb_floor)
    strain = jnp.sum(
        grad_x[:3] * grad_x[:3] + grad_y[:3] * grad_y[:3] + grad_z[:3] * grad_z[:3], axis=0
    )
    produce = eddy_visc * strain
    diffuse = jnp.stack(
        [
            molecular + eddy_visc,
            molecular + eddy_visc,
            molecular + eddy_visc,
            heat_diffuse + eddy_visc / 0.9,
            molecular + eddy_visc,
            molecular + eddy_visc / 1.3,
        ],
        0,
    )
    dissip_source = (
        (prod_coeff * produce - dissip_coeff * dissip) * dissip / jnp.maximum(kinetic, turb_floor)
    )
    source = jnp.concatenate(
        [lorentz, joule[None], (produce - dissip)[None], dissip_source[None]], 0
    )
    return center + time_step * (diffuse * laplace - transport + source)


def flow_step(induction_tables, em_loads):
    padded = extended(induction_tables, (("slab", 1),), 1)
    padded = jnp.pad(padded, ((0, 0), (0, 0), (1, 1), (0, 0)))
    return advance(padded, em_loads[:3], em_loads[3])


def local_coupled(induction_tables, zone_labels, zone_resistivity_inverse):
    conduct = ohmic_admittance(zone_labels, zone_resistivity_inverse, induction_tables[3])
    return jnp.concatenate([reduce_onto_parent(induction_tables[:3]), conduct[None]], 0)


def layered_on_device(
    melt_speeds,
    heat_state,
    eddy_quantities,
    zone_labels,
    zone_resistivity_inverse,
    imposed_induction,
    winding_current,
    window_entry_induction_guess,
):
    induction_tables = jnp.concatenate([melt_speeds, heat_state[None], eddy_quantities], 0)
    arrived = (
        lax.all_to_all(
            window_entry_induction_guess, "slab", split_axis=3, concat_axis=1, tiled=True
        ),
        lax.all_to_all(imposed_induction, "slab", split_axis=3, concat_axis=1, tiled=True),
        lax.all_to_all(winding_current, "slab", split_axis=3, concat_axis=1, tiled=True),
    )
    potential = jnp.transpose(arrived[0], (0, 3, 2, 1))
    field_local = jnp.transpose(arrived[1], (0, 3, 2, 1))
    coil_local = jnp.transpose(arrived[2], (0, 3, 2, 1))
    for step_index in range(STEPS):
        coupled = local_coupled(induction_tables, zone_labels, zone_resistivity_inverse)
        potential, em_loads = relax(coupled, field_local, coil_local, potential)
        induction_tables = flow_step(induction_tables, prolong(em_loads))
    potential = lax.all_to_all(
        jnp.transpose(potential, (0, 3, 2, 1)), "slab", split_axis=1, concat_axis=3, tiled=True
    )
    return (induction_tables[:3], induction_tables[3], induction_tables[4:], potential)


ROW = 8
LANES = 128
MESH = pl.DeviceIdType.MESH


def iota(shape, dim):
    return lax.broadcasted_iota(jnp.int32, shape, dim)


def thirds(value):
    high = value.astype(jnp.bfloat16)
    rest = value - high.astype(jnp.float32)
    middle = rest.astype(jnp.bfloat16)
    low = (rest - middle.astype(jnp.float32)).astype(jnp.bfloat16)
    return high, middle, low


def times_right(value, matrix):
    rows = value.shape[0]
    out = jnp.dot(
        jnp.concatenate(thirds(value), 0), matrix, preferred_element_type=jnp.float32
    )
    return out[:rows] + out[rows : 2 * rows] + out[2 * rows :]


def times_left(matrix, value):
    return jnp.dot(
        jnp.concatenate([matrix] * 3, 1),
        jnp.concatenate(thirds(value), 0),
        preferred_element_type=jnp.float32,
    )


def pairing(shape, fine_dim, scale):
    fine = lax.shift_right_logical(iota(shape, fine_dim), 1)
    return jnp.where(fine == iota(shape, 1 - fine_dim), scale, 0.0).astype(jnp.bfloat16)


def left_roll(value, shift):
    width = value.shape[-1]
    shift = shift % width
    return value if shift == 0 else pltpu.roll(value, width - shift, value.ndim - 1)


def fused_kernel(
    n,
    xl,
    melt_ref,
    heat_ref,
    eddy_ref,
    zone_ref,
    table_ref,
    own_ref,
    vel_out,
    temp_out,
    turb_out,
    pot_out,
    fields0,
    fields1,
    send_f,
    recv_f,
    send_b,
    recv_b,
    halo_out0,
    halo_in0,
    halo_out1,
    halo_in1,
    pot_a,
    pot_b,
    field1,
    field2,
    coil,
    emf,
    source,
    inverse,
    loads,
    zone_sigma,
    load_sem,
    f_send_sem,
    f_recv_sem,
    b_send_sem,
    b_recv_sem,
    p_send_sem,
    p_recv_sem,
    h_send_sem,
    h_recv_sem,
):
    me = lax.axis_index("slab")
    fields = (fields0, fields1)
    halo_out = (halo_out0, halo_out1)
    halo_in = (halo_in0, halo_in1)
    win = xl + 2 * SWEEPS
    depth, rows = own_ref.shape[1:3]
    fine_rows, width = heat_ref.shape[1:]
    body = pl.ds(ROW, fine_rows)
    cols = width // 2
    lane = iota((rows, LANES), 1)
    group = lane // win
    inner = lane % win
    sub = iota((rows, LANES), 0)

    def peer(index):
        return {"slab": index}

    fetches = [
        pltpu.make_async_copy(melt_ref, fields0.at[0:3, 1:3, body, :], load_sem.at[0]),
        pltpu.make_async_copy(heat_ref, fields0.at[3, 1:3, body, :], load_sem.at[1]),
        pltpu.make_async_copy(eddy_ref, fields0.at[4:6, 1:3, body, :], load_sem.at[2]),
    ]
    for fetch in fetches:
        fetch.start()

    barrier = pltpu.get_barrier_semaphore()
    for offset in range(1, n):
        pl.semaphore_signal(
            barrier, inc=1, device_id=peer(lax.rem(me + offset, n)), device_id_type=MESH
        )

    for block in fields:
        edge = jnp.zeros((6, 4, ROW, width), jnp.float32)
        block[:, :, 0:ROW, :] = edge
        block[:, :, ROW + fine_rows :, :] = edge

    @pl.when(me == 0)
    def _():
        for block in fields:
            block[:, 0, body, :] = jnp.zeros((6, fine_rows, width), jnp.float32)
        for block in halo_in:
            block[0] = jnp.zeros(block.shape[1:], jnp.float32)

    @pl.when(me == n - 1)
    def _():
        for block in fields:
            block[:, 3, body, :] = jnp.zeros((6, fine_rows, width), jnp.float32)
        for block in halo_in:
            block[1] = jnp.zeros(block.shape[1:], jnp.float32)

    labels = zone_ref[0]
    sigma0 = jnp.zeros(labels.shape, jnp.float32)
    for region in range(table_ref.shape[0]):
        sigma0 = sigma0 + jnp.where(labels == region, table_ref[region], 0.0)
    zone_sigma[...] = sigma0

    slot = inner // SWEEPS
    for z in range(depth):
        to_left = jnp.zeros((rows, LANES), jnp.float32)
        to_right = to_left
        for a in range(3):
            value = own_ref[a, z]
            to_left = jnp.where(slot == a, left_roll(value, SWEEPS - SWEEPS * a), to_left)
            to_right = jnp.where(slot == a, left_roll(value, xl - SWEEPS * a), to_right)
        halo_out0[0, z] = to_left
        halo_out0[1, z] = to_right

    def plane_copies(step):
        block = fields[step]
        down = pltpu.make_async_remote_copy(
            src_ref=block.at[:, 1, body, :],
            dst_ref=block.at[:, 3, body, :],
            send_sem=p_send_sem.at[step, 0],
            recv_sem=p_recv_sem.at[step, 0],
            device_id=peer(me - 1),
            device_id_type=MESH,
        )
        up = pltpu.make_async_remote_copy(
            src_ref=block.at[:, 2, body, :],
            dst_ref=block.at[:, 0, body, :],
            send_sem=p_send_sem.at[step, 1],
            recv_sem=p_recv_sem.at[step, 1],
            device_id=peer(me + 1),
            device_id_type=MESH,
        )
        return down, up

    def halo_copies(step):
        down = pltpu.make_async_remote_copy(
            src_ref=halo_out[step].at[0],
            dst_ref=halo_in[step].at[1],
            send_sem=h_send_sem.at[step, 0],
            recv_sem=h_recv_sem.at[step, 0],
            device_id=peer(me - 1),
            device_id_type=MESH,
        )
        up = pltpu.make_async_remote_copy(
            src_ref=halo_out[step].at[1],
            dst_ref=halo_in[step].at[0],
            send_sem=h_send_sem.at[step, 1],
            recv_sem=h_recv_sem.at[step, 1],
            device_id=peer(me + 1),
            device_id_type=MESH,
        )
        return down, up

    def start_pair(pair):
        @pl.when(me > 0)
        def _():
            pair[0].start()

        @pl.when(me < n - 1)
        def _():
            pair[1].start()

    def receive_pair(pair):
        @pl.when(me < n - 1)
        def _():
            pair[0].wait_recv()

        @pl.when(me > 0)
        def _():
            pair[1].wait_recv()

    def sent_pair(pair):
        @pl.when(me > 0)
        def _():
            pair[0].wait_send()

        @pl.when(me < n - 1)
        def _():
            pair[1].wait_send()

    def spread(step, send, recv, send_sem, recv_sem):
        copies = []
        for offset in range(1, n):
            target = lax.rem(me + offset, n)
            copies.append(
                pltpu.make_async_remote_copy(
                    src_ref=send.at[step, target],
                    dst_ref=recv.at[step, me],
                    send_sem=send_sem.at[step, offset],
                    recv_sem=recv_sem.at[step, offset],
                    device_id=peer(target),
                    device_id_type=MESH,
                )
            )
        return copies

    halve_rows = pairing((4 * rows, 4 * fine_rows), 1, 0.125)
    halve_cols = pairing((2 * LANES, LANES), 0, 1.0)
    double_rows = pairing((4 * fine_rows, 4 * rows), 0, 1.0)
    double_cols = pairing((LANES, 2 * LANES), 1, 1.0)

    def restrict_and_window(step):
        block = fields[step]
        parts = [block[f, 1, body, :] + block[f, 2, body, :] for f in range(3)]
        parts.append(
            jnp.exp(-thermal_gradient_factor * block[3, 1, body, :])
            + jnp.exp(-thermal_gradient_factor * block[3, 2, body, :])
        )
        short = times_left(halve_rows, jnp.concatenate(parts, 0))
        coarse = jnp.concatenate(
            [
                times_right(short[:, at : at + 2 * LANES], halve_cols)
                for at in range(0, width, 2 * LANES)
            ],
            1,
        )
        comps = [coarse[c * rows : (c + 1) * rows] for c in range(4)]
        comps[3] = comps[3] * zone_sigma[...]
        for target in range(n):
            first = target * xl - SWEEPS
            message = jnp.zeros((rows, LANES), jnp.float32)
            for c in range(4):
                moved = left_roll(comps[c], first - c * win)[:, :LANES]
                message = jnp.where(group == c, moved, message)
            send_f[step, target] = message

    def turned(value):
        return left_roll(value, win), left_roll(value, 2 * win), left_roll(value, 3 * win)

    def relax_all(step):
        x_at = me * xl - SWEEPS + inner
        valid = (x_at >= 0) & (x_at < cols) & (group < 3)

        def prepare(z, carry):
            value = recv_f[step, z]
            one, two, three = turned(value)
            next_comp = jnp.where(group < 2, one, two)
            last_comp = jnp.where(group == 0, two, three)
            sigma = jnp.where(group == 0, three, jnp.where(group == 1, two, one))
            motional = next_comp * field2[z] - last_comp * field1[z]
            emf[z] = motional
            source[z] = sigma * motional + coil[z]
            inverse[z] = jnp.where(valid, 1.0 / (6.0 + coupling * sigma), 0.0)
            return carry

        lax.fori_loop(0, depth, prepare, 0)

        def sweep(old, new):
            for z in range(depth):
                centre = old[z + 1]
                total = source[z] + old[z] + old[z + 2]
                total = total + left_roll(centre, 1) + left_roll(centre, LANES - 1)
                total = total + jnp.where(sub == 0, 0.0, pltpu.roll(centre, 1, 0))
                total = total + jnp.where(sub == rows - 1, 0.0, pltpu.roll(centre, rows - 1, 0))
                new[z + 1] = total * inverse[z]

        def two_sweeps(index, carry):
            sweep(pot_a, pot_b)
            sweep(pot_b, pot_a)
            return carry

        lax.fori_loop(0, SWEEPS // 2, two_sweeps, 0)

        half = rows // 2
        packed = iota((half, LANES), 1) // xl

        def load(z, carry):
            value = recv_f[step, z]
            one, two, three = turned(value)
            sigma = jnp.where(group == 0, three, jnp.where(group == 1, two, one))
            drive = emf[z] - coupling * pot_a[z + 1]
            current = sigma * drive + coil[z]
            one, two, three = turned(current)
            next_comp = jnp.where(group < 2, one, two)
            last_comp = jnp.where(group == 0, two, three)
            force = next_comp * field2[z] - last_comp * field1[z]
            one, two, three = turned(drive * drive)
            both = jnp.where(group == 3, value * (one + two + three), force)
            message = jnp.zeros((half, LANES), jnp.float32)
            for h in range(2):
                piece = both[h * half : (h + 1) * half]
                for c in range(4):
                    at = 4 * h + c
                    moved = left_roll(piece, c * win + SWEEPS - at * xl)
                    message = jnp.where(packed == at, moved, message)
            send_b[step, z] = message
            return carry

        lax.fori_loop(0, depth, load, 0)

    def prolong_loads(step):
        half = rows // 2
        packed = iota((half, LANES), 1) // xl
        per = LANES // xl
        strips = []
        for c in range(4):
            for h in range(2):
                strip = []
                for first in range(0, n, per):
                    piece = jnp.zeros((half, LANES), jnp.float32)
                    for d in range(per):
                        moved = left_roll(recv_b[step, first + d], (4 * h + c - d) * xl)
                        piece = jnp.where(packed == d, moved, piece)
                    strip.append(piece)
                strips.append(jnp.concatenate(strip, 1))
        coarse = jnp.concatenate(strips, 0)
        wide = jnp.concatenate(
            [
                times_right(coarse[:, at : at + LANES], double_cols)
                for at in range(0, cols, LANES)
            ],
            1,
        )
        loads[...] = times_left(double_rows, wide)

    def advance_all(step, store):
        block = fields[step]
        sub8 = iota((ROW, width), 0)
        lane8 = iota((ROW, width), 1)

        def chunk(plane, index, carry):
            low = pl.multiple_of(index * ROW, ROW)
            at = pl.multiple_of(index * ROW + ROW, ROW)
            high = pl.multiple_of(index * ROW + 2 * ROW, ROW)
            here = pl.ds(at, ROW)
            centre = [block[f, plane, here, :] for f in range(6)]
            kinetic, dissip = centre[4], centre[5]
            eddy = eddy_coeff * kinetic * kinetic / jnp.maximum(dissip, turb_floor)
            diffuse = molecular + eddy
            strain = None
            for f in range(6):
                mid = centre[f]
                z_minus = block[f, plane - 1, here, :]
                z_plus = block[f, plane + 1, here, :]
                before = block[f, plane, pl.ds(low, ROW), :]
                after = block[f, plane, pl.ds(high, ROW), :]
                y_minus = pltpu.roll(jnp.where(sub8 == ROW - 1, before, mid), 1, 0)
                y_plus = pltpu.roll(jnp.where(sub8 == 0, after, mid), ROW - 1, 0)
                x_minus = jnp.where(lane8 == 0, 0.0, pltpu.roll(mid, 1, 1))
                x_plus = jnp.where(lane8 == width - 1, 0.0, pltpu.roll(mid, width - 1, 1))
                laplace = (
                    (z_plus + z_minus) + (y_plus + y_minus) + (x_plus + x_minus) - 6.0 * mid
                )
                grad_z = 0.5 * (z_plus - z_minus)
                grad_y = 0.5 * (y_plus - y_minus)
                grad_x = 0.5 * (x_plus - x_minus)
                transport = centre[0] * grad_x + centre[1] * grad_y + centre[2] * grad_z
                if f < 3:
                    square = grad_x * grad_x + grad_y * grad_y + grad_z * grad_z
                    strain = square if strain is None else strain + square
                if f < 4:
                    src = loads[pl.ds(pl.multiple_of(f * fine_rows + index * ROW, ROW), ROW), :]
                elif f == 4:
                    produce = eddy * strain
                    src = produce - dissip
                else:
                    src = (
                        (prod_coeff * produce - dissip_coeff * dissip)
                        * dissip
                        / jnp.maximum(kinetic, turb_floor)
                    )
                if f == 3:
                    spread_by = heat_diffuse + eddy * (1.0 / 0.9)
                elif f == 5:
                    spread_by = molecular + eddy * (1.0 / 1.3)
                else:
                    spread_by = diffuse
                store(
                    f, plane, index, mid + time_step * (spread_by * laplace - transport + src)
                )
            return carry

        for plane in (1, 2):
            lax.fori_loop(0, fine_rows // ROW, functools.partial(chunk, plane), 0)

    def store_mid(f, plane, index, value):
        fields1[f, plane, pl.ds(pl.multiple_of(index * ROW + ROW, ROW), ROW), :] = value

    def store_last(f, plane, index, value):
        here = pl.ds(pl.multiple_of(index * ROW, ROW), ROW)
        if f < 3:
            vel_out[f, plane - 1, here, :] = value
        elif f == 3:
            temp_out[plane - 1, here, :] = value
        else:
            turb_out[f - 4, plane - 1, here, :] = value

    pack = win // SWEEPS

    def pack_potential():
        for z in range(0, depth, pack):
            to_left = jnp.zeros((rows, LANES), jnp.float32)
            to_right = to_left
            for k in range(pack):
                value = pot_a[z + k + 1]
                to_left = jnp.where(slot == k, left_roll(value, SWEEPS - SWEEPS * k), to_left)
                to_right = jnp.where(slot == k, left_roll(value, xl - SWEEPS * k), to_right)
            halo_out1[0, z // pack] = to_left
            halo_out1[1, z // pack] = to_right

    def framed(own, from_left, from_right, k):
        left = left_roll(from_left, SWEEPS * k)
        right = left_roll(from_right, SWEEPS * k - (win - SWEEPS))
        whole = jnp.where(
            inner < SWEEPS, left, jnp.where(inner >= win - SWEEPS, right, own)
        )
        return jnp.where(group < 3, whole, 0.0)

    for step in range(STEPS):
        if step == 0:
            for fetch in fetches:
                fetch.wait()
        restrict_and_window(step)
        if step == 0:
            pl.semaphore_wait(barrier, n - 1)
        forward = spread(step, send_f, recv_f, f_send_sem, f_recv_sem)
        for copy in forward:
            copy.start()
        if step == 0:
            halos = halo_copies(0)
            start_pair(halos)
        planes = plane_copies(step)
        start_pair(planes)
        recv_f[step, me] = send_f[step, me]
        if step == 0:
            pot_a[0] = jnp.zeros((rows, LANES), jnp.float32)
            pot_a[depth + 1] = jnp.zeros((rows, LANES), jnp.float32)
            pot_b[0] = jnp.zeros((rows, LANES), jnp.float32)
            pot_b[depth + 1] = jnp.zeros((rows, LANES), jnp.float32)
        receive_pair(halos)
        if step == 0:
            for z in range(depth):
                sides = halo_in0[0, z], halo_in0[1, z]
                pot_a[z + 1] = framed(own_ref[0, z], *sides, 0)
                one, two, three = turned(framed(own_ref[1, z], *sides, 1))
                field1[z] = jnp.where(group < 2, one, two)
                field2[z] = jnp.where(group == 0, two, three)
                coil[z] = framed(own_ref[2, z], *sides, 2)
        else:
            for z in range(depth):
                sides = halo_in1[0, z // pack], halo_in1[1, z // pack]
                pot_a[z + 1] = framed(pot_a[z + 1], *sides, z % pack)
        sent_pair(halos)
        for copy in forward:
            copy.wait_recv()
        relax_all(step)
        back = spread(step, send_b, recv_b, b_send_sem, b_recv_sem)
        for copy in back:
            copy.start()
        recv_b[step, me] = send_b[step, me]
        if step == 0:
            pack_potential()
            halos = halo_copies(1)
            start_pair(halos)
        else:
            pot_out[...] = pot_a[1 : depth + 1]
        for copy in forward:
            copy.wait_send()
        for copy in back:
            copy.wait_recv()
        prolong_loads(step)
        receive_pair(planes)
        advance_all(step, store_mid if step == 0 else store_last)
        for copy in back:
            copy.wait_send()
        sent_pair(planes)


def fused_on_device(
    melt_speeds,
    heat_state,
    eddy_quantities,
    zone_labels,
    zone_resistivity_inverse,
    imposed_induction,
    winding_current,
    window_entry_induction_guess,
):
    n = lax.axis_size("slab")
    _, xl, rows, depth = imposed_induction.shape
    _, fine_rows, width = heat_state.shape
    win = xl + 2 * SWEEPS
    own = jnp.stack([window_entry_induction_guess, imposed_induction, winding_current])
    own = jnp.transpose(own, (0, 4, 3, 1, 2))
    own = jnp.pad(own, ((0, 0), (0, 0), (0, 0), (0, 1), (SWEEPS, SWEEPS)))
    own = own.reshape(3, depth, rows, 4 * win)

    def vmem(*shape):
        return pltpu.VMEM(shape, jnp.float32)

    plane = (depth, rows, LANES)
    dma = pltpu.SemaphoreType.DMA
    whole = pl.BlockSpec(memory_space=pltpu.VMEM)
    anywhere = pl.BlockSpec(memory_space=pl.ANY)
    vel, temp, turb, pot = pl.pallas_call(
        functools.partial(fused_kernel, n, xl),
        out_shape=(
            jax.ShapeDtypeStruct(melt_speeds.shape, jnp.float32),
            jax.ShapeDtypeStruct(heat_state.shape, jnp.float32),
            jax.ShapeDtypeStruct(eddy_quantities.shape, jnp.float32),
            jax.ShapeDtypeStruct(plane, jnp.float32),
        ),
        in_specs=[
            anywhere,
            anywhere,
            anywhere,
            whole,
            pl.BlockSpec(memory_space=pltpu.SMEM),
            whole,
        ],
        out_specs=(whole,) * 4,
        scratch_shapes=[
            vmem(6, 4, fine_rows + 2 * ROW, width),
            vmem(6, 4, fine_rows + 2 * ROW, width),
            vmem(STEPS, n, rows, LANES),
            vmem(STEPS, n, rows, LANES),
            vmem(STEPS, n, rows // 2, LANES),
            vmem(STEPS, n, rows // 2, LANES),
            vmem(2, *plane),
            vmem(2, *plane),
            vmem(2, depth * SWEEPS // win, rows, LANES),
            vmem(2, depth * SWEEPS // win, rows, LANES),
            vmem(depth + 2, rows, LANES),
            vmem(depth + 2, rows, LANES),
            vmem(*plane),
            vmem(*plane),
            vmem(*plane),
            vmem(*plane),
            vmem(*plane),
            vmem(*plane),
            vmem(4 * fine_rows, width),
            vmem(rows, width // 2),
            dma((3,)),
            dma((STEPS, n)),
            dma((STEPS, n)),
            dma((STEPS, n)),
            dma((STEPS, n)),
            dma((STEPS, 2)),
            dma((STEPS, 2)),
            dma((STEPS, 2)),
            dma((STEPS, 2)),
        ],
        compiler_params=pltpu.CompilerParams(
            collective_id=0, has_side_effects=True, vmem_limit_bytes=40 * 1024 * 1024
        ),
    )(melt_speeds, heat_state, eddy_quantities, zone_labels, zone_resistivity_inverse, own)
    pot = pot.reshape(depth, rows, 4, win)[:, :, :3, SWEEPS : SWEEPS + xl]
    return vel, temp, turb, jnp.transpose(pot, (2, 3, 1, 0))


def fits_fused(n, heat_state, imposed_induction):
    _, xl, rows, depth = imposed_induction.shape
    planes, fine_rows, width = heat_state.shape
    win = xl + 2 * SWEEPS
    return (
        STEPS == 2
        and SWEEPS % 2 == 0
        and n > 1
        and planes == 2
        and depth == n
        and rows == 2 * ROW
        and fine_rows == 2 * rows
        and width == 2 * n * xl
        and width % (4 * LANES) == 0
        and 4 * win == LANES
        and xl == 2 * SWEEPS
        and n % (LANES // xl) == 0
        and depth % (win // SWEEPS) == 0
    )


def on_device(*args):
    if fits_fused(lax.axis_size("slab"), args[1], args[5]):
        return fused_on_device(*args)
    return layered_on_device(*args)


def solution(mesh):
    return jax.shard_map(
        on_device,
        mesh=mesh,
        in_specs=(
            P(None, ("groups", "slab"), None, None),
            P(("groups", "slab"), None, None),
            P(None, ("groups", "slab"), None, None),
            P(("groups", "slab"), None, None),
            P(),
            P(None, ("groups", "slab"), None, None),
            P(None, ("groups", "slab"), None, None),
            P(None, ("groups", "slab"), None, None),
        ),
        out_specs=(
            P(None, ("groups", "slab"), None, None),
            P(("groups", "slab"), None, None),
            P(None, ("groups", "slab"), None, None),
            P(None, ("groups", "slab"), None, None),
        ),
        check_vma=False,
    )
```

```python
import functools

import jax
import jax.numpy as jnp
from jax import lax
from jax.experimental import pallas as pl
from jax.experimental.pallas import tpu as pltpu
from jax.sharding import PartitionSpec as P

STEPS = 2
SWEEPS = 8


time_step = 0.02
molecular = 0.01
heat_diffuse = 0.01
eddy_coeff = 0.09
prod_coeff = 1.44
dissip_coeff = 1.92
turb_floor = 0.05
coupling = 1.0
thermal_gradient_factor = 0.3


def extended(block, sides, width):
    for axis, dim in sides:
        count = lax.axis_size(axis)
        forward = [(i, i + 1) for i in range(count - 1)]
        backward = [(target, source) for source, target in forward]
        low = lax.ppermute(
            lax.slice_in_dim(block, block.shape[dim] - width, None, axis=dim), axis, forward
        )
        high = lax.ppermute(lax.slice_in_dim(block, 0, width, axis=dim), axis, backward)
        block = jnp.concatenate([low, block, high], axis=dim)
    return block


def reduce_onto_parent(block):
    comps, depth, rows, cols = block.shape
    shaped = block.reshape(comps, depth // 2, 2, rows // 2, 2, cols // 2, 2)
    return jnp.mean(shaped, axis=(2, 4, 6))


def prolong(block):
    comps, depth, rows, cols = block.shape
    wide = jnp.broadcast_to(
        block[:, :, None, :, None, :, None], (comps, depth, 2, rows, 2, cols, 2)
    )
    return wide.reshape(comps, depth * 2, rows * 2, cols * 2)


def cross(left_vec, right_vec):
    return jnp.stack(
        [
            left_vec[1] * right_vec[2] - left_vec[2] * right_vec[1],
            left_vec[2] * right_vec[0] - left_vec[0] * right_vec[2],
            left_vec[0] * right_vec[1] - left_vec[1] * right_vec[0],
        ],
        0,
    )


def neighbours(padded):
    return (
        padded[:, 2:, 1:-1, 1:-1]
        + padded[:, :-2, 1:-1, 1:-1]
        + padded[:, 1:-1, 2:, 1:-1]
        + padded[:, 1:-1, :-2, 1:-1]
        + padded[:, 1:-1, 1:-1, 2:]
        + padded[:, 1:-1, 1:-1, :-2]
    )


def ohmic_admittance(zone_labels, zone_resistivity_inverse, heat_state):
    labels = jnp.arange(zone_resistivity_inverse.shape[0], dtype=jnp.int32)
    onehot = zone_labels[None] == labels[:, None, None, None]
    searched_higher = jnp.sum(
        jnp.where(onehot, zone_resistivity_inverse[:, None, None, None], jnp.float32(0.0)), axis=0
    )
    return (
        searched_higher
        * reduce_onto_parent(jnp.exp(-thermal_gradient_factor * heat_state)[None])[0]
    )


def faces(potential):
    padded = extended(potential, (("slab", 1),), 1)
    return jnp.pad(padded, ((0, 0), (0, 0), (1, 1), (1, 1)))


def relax(coupled, imposed_induction, winding_current, potential):
    conduct = coupled[3]
    motional = cross(coupled[:3], imposed_induction)
    source = conduct * motional + winding_current
    diagonal = 6.0 + coupling * conduct
    for sweep_index in range(SWEEPS):
        potential = (source + neighbours(faces(potential))) / diagonal
    drive_field = motional - coupling * potential
    current = conduct * drive_field + winding_current
    lorentz = cross(current, imposed_induction)
    joule = conduct * jnp.sum(drive_field * drive_field, axis=0)
    return (potential, jnp.concatenate([lorentz, joule[None]], 0))


def advance(padded, lorentz, joule):
    bordered = jnp.pad(padded, ((0, 0), (0, 0), (0, 0), (1, 1)))
    center = bordered[:, 1:-1, 1:-1, 1:-1]
    z_plus = bordered[:, 2:, 1:-1, 1:-1]
    z_minus = bordered[:, :-2, 1:-1, 1:-1]
    y_plus = bordered[:, 1:-1, 2:, 1:-1]
    y_minus = bordered[:, 1:-1, :-2, 1:-1]
    x_plus = bordered[:, 1:-1, 1:-1, 2:]
    x_minus = bordered[:, 1:-1, 1:-1, :-2]
    grad_z = 0.5 * (z_plus - z_minus)
    grad_y = 0.5 * (y_plus - y_minus)
    grad_x = 0.5 * (x_plus - x_minus)
    laplace = z_plus + z_minus + y_plus + y_minus + x_plus + x_minus - 6.0 * center
    kinetic = center[4]
    dissip = center[5]
    transport = center[0] * grad_x + center[1] * grad_y + center[2] * grad_z
    eddy_visc = eddy_coeff * kinetic * kinetic / jnp.maximum(dissip, turb_floor)
    strain = jnp.sum(
        grad_x[:3] * grad_x[:3] + grad_y[:3] * grad_y[:3] + grad_z[:3] * grad_z[:3], axis=0
    )
    produce = eddy_visc * strain
    diffuse = jnp.stack(
        [
            molecular + eddy_visc,
            molecular + eddy_visc,
            molecular + eddy_visc,
            heat_diffuse + eddy_visc / 0.9,
            molecular + eddy_visc,
            molecular + eddy_visc / 1.3,
        ],
        0,
    )
    dissip_source = (
        (prod_coeff * produce - dissip_coeff * dissip) * dissip / jnp.maximum(kinetic, turb_floor)
    )
    source = jnp.concatenate(
        [lorentz, joule[None], (produce - dissip)[None], dissip_source[None]], 0
    )
    return center + time_step * (diffuse * laplace - transport + source)


def flow_step(induction_tables, em_loads):
    padded = extended(induction_tables, (("slab", 1),), 1)
    padded = jnp.pad(padded, ((0, 0), (0, 0), (1, 1), (0, 0)))
    return advance(padded, em_loads[:3], em_loads[3])


def local_coupled(induction_tables, zone_labels, zone_resistivity_inverse):
    conduct = ohmic_admittance(zone_labels, zone_resistivity_inverse, induction_tables[3])
    return jnp.concatenate([reduce_onto_parent(induction_tables[:3]), conduct[None]], 0)


def layered_on_device(
    melt_speeds,
    heat_state,
    eddy_quantities,
    zone_labels,
    zone_resistivity_inverse,
    imposed_induction,
    winding_current,
    window_entry_induction_guess,
):
    induction_tables = jnp.concatenate([melt_speeds, heat_state[None], eddy_quantities], 0)
    arrived = (
        lax.all_to_all(
            window_entry_induction_guess, "slab", split_axis=3, concat_axis=1, tiled=True
        ),
        lax.all_to_all(imposed_induction, "slab", split_axis=3, concat_axis=1, tiled=True),
        lax.all_to_all(winding_current, "slab", split_axis=3, concat_axis=1, tiled=True),
    )
    potential = jnp.transpose(arrived[0], (0, 3, 2, 1))
    field_local = jnp.transpose(arrived[1], (0, 3, 2, 1))
    coil_local = jnp.transpose(arrived[2], (0, 3, 2, 1))
    for step_index in range(STEPS):
        coupled = local_coupled(induction_tables, zone_labels, zone_resistivity_inverse)
        potential, em_loads = relax(coupled, field_local, coil_local, potential)
        induction_tables = flow_step(induction_tables, prolong(em_loads))
    potential = lax.all_to_all(
        jnp.transpose(potential, (0, 3, 2, 1)), "slab", split_axis=1, concat_axis=3, tiled=True
    )
    return (induction_tables[:3], induction_tables[3], induction_tables[4:], potential)


ROW = 8
LANES = 128
MESH = pl.DeviceIdType.MESH


def iota(shape, dim):
    return lax.broadcasted_iota(jnp.int32, shape, dim)


def thirds(value):
    high = value.astype(jnp.bfloat16)
    rest = value - high.astype(jnp.float32)
    middle = rest.astype(jnp.bfloat16)
    low = (rest - middle.astype(jnp.float32)).astype(jnp.bfloat16)
    return high, middle, low


def times_right(value, matrix):
    rows = value.shape[0]
    out = jnp.dot(
        jnp.concatenate(thirds(value), 0), matrix, preferred_element_type=jnp.float32
    )
    return out[:rows] + out[rows : 2 * rows] + out[2 * rows :]


def times_left(matrix, value):
    return jnp.dot(
        jnp.concatenate([matrix] * 3, 1),
        jnp.concatenate(thirds(value), 0),
        preferred_element_type=jnp.float32,
    )


def pairing(shape, fine_dim, scale):
    fine = lax.shift_right_logical(iota(shape, fine_dim), 1)
    return jnp.where(fine == iota(shape, 1 - fine_dim), scale, 0.0).astype(jnp.bfloat16)


def left_roll(value, shift):
    width = value.shape[-1]
    shift = shift % width
    return value if shift == 0 else pltpu.roll(value, width - shift, value.ndim - 1)


def fused_kernel(
    n,
    xl,
    melt_ref,
    heat_ref,
    eddy_ref,
    zone_ref,
    table_ref,
    guess_ref,
    induction_ref,
    winding_ref,
    vel_out,
    temp_out,
    turb_out,
    pot_out,
    fields0,
    fields1,
    send_f,
    recv_f,
    send_b,
    recv_b,
    own_ref,
    halo_out0,
    halo_in0,
    halo_out1,
    halo_in1,
    pot_a,
    pot_b,
    field1,
    field2,
    coil,
    emf,
    source,
    inverse,
    loads,
    zone_sigma,
    load_sem,
    f_send_sem,
    f_recv_sem,
    b_send_sem,
    b_recv_sem,
    p_send_sem,
    p_recv_sem,
    h_send_sem,
    h_recv_sem,
):
    me = lax.axis_index("slab")
    fields = (fields0, fields1)
    halo_out = (halo_out0, halo_out1)
    halo_in = (halo_in0, halo_in1)
    win = xl + 2 * SWEEPS
    depth, rows = guess_ref.shape[1:3]
    fine_rows, width = heat_ref.shape[1:]
    body = pl.ds(ROW, fine_rows)
    cols = width // 2
    lane = iota((rows, LANES), 1)
    group = lane // win
    inner = lane % win
    sub = iota((rows, LANES), 0)

    def peer(index):
        return {"slab": index}

    fetches = [
        pltpu.make_async_copy(melt_ref, fields0.at[0:3, 1:3, body, :], load_sem.at[0]),
        pltpu.make_async_copy(heat_ref, fields0.at[3, 1:3, body, :], load_sem.at[1]),
        pltpu.make_async_copy(eddy_ref, fields0.at[4:6, 1:3, body, :], load_sem.at[2]),
    ]
    for fetch in fetches:
        fetch.start()

    barrier = pltpu.get_barrier_semaphore()
    for offset in range(1, n):
        pl.semaphore_signal(
            barrier, inc=1, device_id=peer(lax.rem(me + offset, n)), device_id_type=MESH
        )

    for block in fields:
        edge = jnp.zeros((6, 4, ROW, width), jnp.float32)
        block[:, :, 0:ROW, :] = edge
        block[:, :, ROW + fine_rows :, :] = edge

    @pl.when(me == 0)
    def _():
        for block in fields:
            block[:, 0, body, :] = jnp.zeros((6, fine_rows, width), jnp.float32)
        for block in halo_in:
            block[0] = jnp.zeros(block.shape[1:], jnp.float32)

    @pl.when(me == n - 1)
    def _():
        for block in fields:
            block[:, 3, body, :] = jnp.zeros((6, fine_rows, width), jnp.float32)
        for block in halo_in:
            block[1] = jnp.zeros(block.shape[1:], jnp.float32)

    labels = zone_ref[0]
    sigma0 = jnp.zeros(labels.shape, jnp.float32)
    for region in range(table_ref.shape[0]):
        sigma0 = sigma0 + jnp.where(labels == region, table_ref[region], 0.0)
    zone_sigma[...] = sigma0

    def blank(lanes):
        return jnp.zeros((rows, lanes), jnp.float32)

    for a, coarse_ref in enumerate((guess_ref, induction_ref, winding_ref)):
        for z in range(depth):
            own_ref[a, z] = jnp.concatenate(
                [
                    blank(SWEEPS),
                    coarse_ref[0, z],
                    blank(2 * SWEEPS),
                    coarse_ref[1, z],
                    blank(2 * SWEEPS),
                    coarse_ref[2, z],
                    blank(SWEEPS + win),
                ],
                1,
            )

    slot = inner // SWEEPS
    for z in range(depth):
        to_left = jnp.zeros((rows, LANES), jnp.float32)
        to_right = to_left
        for a in range(3):
            value = own_ref[a, z]
            to_left = jnp.where(slot == a, left_roll(value, SWEEPS - SWEEPS * a), to_left)
            to_right = jnp.where(slot == a, left_roll(value, xl - SWEEPS * a), to_right)
        halo_out0[0, z] = to_left
        halo_out0[1, z] = to_right

    def plane_copies(step):
        block = fields[step]
        down = pltpu.make_async_remote_copy(
            src_ref=block.at[:, 1, body, :],
            dst_ref=block.at[:, 3, body, :],
            send_sem=p_send_sem.at[step, 0],
            recv_sem=p_recv_sem.at[step, 0],
            device_id=peer(me - 1),
            device_id_type=MESH,
        )
        up = pltpu.make_async_remote_copy(
            src_ref=block.at[:, 2, body, :],
            dst_ref=block.at[:, 0, body, :],
            send_sem=p_send_sem.at[step, 1],
            recv_sem=p_recv_sem.at[step, 1],
            device_id=peer(me + 1),
            device_id_type=MESH,
        )
        return down, up

    def halo_copies(step):
        down = pltpu.make_async_remote_copy(
            src_ref=halo_out[step].at[0],
            dst_ref=halo_in[step].at[1],
            send_sem=h_send_sem.at[step, 0],
            recv_sem=h_recv_sem.at[step, 0],
            device_id=peer(me - 1),
            device_id_type=MESH,
        )
        up = pltpu.make_async_remote_copy(
            src_ref=halo_out[step].at[1],
            dst_ref=halo_in[step].at[0],
            send_sem=h_send_sem.at[step, 1],
            recv_sem=h_recv_sem.at[step, 1],
            device_id=peer(me + 1),
            device_id_type=MESH,
        )
        return down, up

    def start_pair(pair):
        @pl.when(me > 0)
        def _():
            pair[0].start()

        @pl.when(me < n - 1)
        def _():
            pair[1].start()

    def receive_pair(pair):
        @pl.when(me < n - 1)
        def _():
            pair[0].wait_recv()

        @pl.when(me > 0)
        def _():
            pair[1].wait_recv()

    def sent_pair(pair):
        @pl.when(me > 0)
        def _():
            pair[0].wait_send()

        @pl.when(me < n - 1)
        def _():
            pair[1].wait_send()

    def spread(step, send, recv, send_sem, recv_sem):
        copies = []
        for offset in range(1, n):
            target = lax.rem(me + offset, n)
            copies.append(
                pltpu.make_async_remote_copy(
                    src_ref=send.at[step, target],
                    dst_ref=recv.at[step, me],
                    send_sem=send_sem.at[step, offset],
                    recv_sem=recv_sem.at[step, offset],
                    device_id=peer(target),
                    device_id_type=MESH,
                )
            )
        return copies

    halve_rows = pairing((4 * rows, 4 * fine_rows), 1, 0.125)
    halve_cols = pairing((2 * LANES, LANES), 0, 1.0)
    double_rows = pairing((4 * fine_rows, 4 * rows), 0, 1.0)
    double_cols = pairing((LANES, 2 * LANES), 1, 1.0)

    def restrict_and_window(step):
        block = fields[step]
        parts = [block[f, 1, body, :] + block[f, 2, body, :] for f in range(3)]
        parts.append(
            jnp.exp(-thermal_gradient_factor * block[3, 1, body, :])
            + jnp.exp(-thermal_gradient_factor * block[3, 2, body, :])
        )
        short = times_left(halve_rows, jnp.concatenate(parts, 0))
        coarse = jnp.concatenate(
            [
                times_right(short[:, at : at + 2 * LANES], halve_cols)
                for at in range(0, width, 2 * LANES)
            ],
            1,
        )
        comps = [coarse[c * rows : (c + 1) * rows] for c in range(4)]
        comps[3] = comps[3] * zone_sigma[...]
        for target in range(n):
            first = target * xl - SWEEPS
            message = jnp.zeros((rows, LANES), jnp.float32)
            for c in range(4):
                moved = left_roll(comps[c], first - c * win)[:, :LANES]
                message = jnp.where(group == c, moved, message)
            send_f[step, target] = message

    def turned(value):
        return left_roll(value, win), left_roll(value, 2 * win), left_roll(value, 3 * win)

    def relax_all(step):
        x_at = me * xl - SWEEPS + inner
        valid = (x_at >= 0) & (x_at < cols) & (group < 3)

        def prepare(z):
            value = recv_f[step, z]
            one, two, three = turned(value)
            next_comp = jnp.where(group < 2, one, two)
            last_comp = jnp.where(group == 0, two, three)
            sigma = jnp.where(group == 0, three, jnp.where(group == 1, two, one))
            motional = next_comp * field2[z] - last_comp * field1[z]
            emf[z] = motional
            source[z] = sigma * motional + coil[z]
            inverse[z] = jnp.where(valid, 1.0 / (6.0 + coupling * sigma), 0.0)

        for z in range(depth):
            prepare(z)

        def sweep(old, new):
            for z in range(depth):
                centre = old[z + 1]
                total = source[z] + old[z] + old[z + 2]
                total = total + left_roll(centre, 1) + left_roll(centre, LANES - 1)
                total = total + jnp.where(sub == 0, 0.0, pltpu.roll(centre, 1, 0))
                total = total + jnp.where(sub == rows - 1, 0.0, pltpu.roll(centre, rows - 1, 0))
                new[z + 1] = total * inverse[z]

        def two_sweeps(index, carry):
            sweep(pot_a, pot_b)
            sweep(pot_b, pot_a)
            return carry

        lax.fori_loop(0, SWEEPS // 2, two_sweeps, 0)

        half = rows // 2
        packed = iota((half, LANES), 1) // xl

        def load(z):
            value = recv_f[step, z]
            one, two, three = turned(value)
            sigma = jnp.where(group == 0, three, jnp.where(group == 1, two, one))
            drive = emf[z] - coupling * pot_a[z + 1]
            current = sigma * drive + coil[z]
            one, two, three = turned(current)
            next_comp = jnp.where(group < 2, one, two)
            last_comp = jnp.where(group == 0, two, three)
            force = next_comp * field2[z] - last_comp * field1[z]
            one, two, three = turned(drive * drive)
            both = jnp.where(group == 3, value * (one + two + three), force)
            message = jnp.zeros((half, LANES), jnp.float32)
            for h in range(2):
                piece = both[h * half : (h + 1) * half]
                for c in range(4):
                    at = 4 * h + c
                    moved = left_roll(piece, c * win + SWEEPS - at * xl)
                    message = jnp.where(packed == at, moved, message)
            send_b[step, z] = message

        for z in range(depth):
            load(z)

    def prolong_loads(step):
        half = rows // 2
        packed = iota((half, LANES), 1) // xl
        per = LANES // xl
        strips = []
        for c in range(4):
            for h in range(2):
                strip = []
                for first in range(0, n, per):
                    piece = jnp.zeros((half, LANES), jnp.float32)
                    for d in range(per):
                        moved = left_roll(recv_b[step, first + d], (4 * h + c - d) * xl)
                        piece = jnp.where(packed == d, moved, piece)
                    strip.append(piece)
                strips.append(jnp.concatenate(strip, 1))
        coarse = jnp.concatenate(strips, 0)
        wide = jnp.concatenate(
            [
                times_right(coarse[:, at : at + LANES], double_cols)
                for at in range(0, cols, LANES)
            ],
            1,
        )
        loads[...] = times_left(double_rows, wide)

    def advance_all(step, store):
        block = fields[step]
        sub8 = iota((ROW, width), 0)
        lane8 = iota((ROW, width), 1)

        def chunk(plane, index, carry):
            low = pl.multiple_of(index * ROW, ROW)
            at = pl.multiple_of(index * ROW + ROW, ROW)
            high = pl.multiple_of(index * ROW + 2 * ROW, ROW)
            here = pl.ds(at, ROW)
            centre = [block[f, plane, here, :] for f in range(6)]
            kinetic, dissip = centre[4], centre[5]
            eddy = eddy_coeff * kinetic * kinetic / jnp.maximum(dissip, turb_floor)
            diffuse = molecular + eddy
            strain = None
            for f in range(6):
                mid = centre[f]
                z_minus = block[f, plane - 1, here, :]
                z_plus = block[f, plane + 1, here, :]
                before = block[f, plane, pl.ds(low, ROW), :]
                after = block[f, plane, pl.ds(high, ROW), :]
                y_minus = pltpu.roll(jnp.where(sub8 == ROW - 1, before, mid), 1, 0)
                y_plus = pltpu.roll(jnp.where(sub8 == 0, after, mid), ROW - 1, 0)
                x_minus = jnp.where(lane8 == 0, 0.0, pltpu.roll(mid, 1, 1))
                x_plus = jnp.where(lane8 == width - 1, 0.0, pltpu.roll(mid, width - 1, 1))
                laplace = (
                    (z_plus + z_minus) + (y_plus + y_minus) + (x_plus + x_minus) - 6.0 * mid
                )
                grad_z = 0.5 * (z_plus - z_minus)
                grad_y = 0.5 * (y_plus - y_minus)
                grad_x = 0.5 * (x_plus - x_minus)
                transport = centre[0] * grad_x + centre[1] * grad_y + centre[2] * grad_z
                if f < 3:
                    square = grad_x * grad_x + grad_y * grad_y + grad_z * grad_z
                    strain = square if strain is None else strain + square
                if f < 4:
                    src = loads[pl.ds(pl.multiple_of(f * fine_rows + index * ROW, ROW), ROW), :]
                elif f == 4:
                    produce = eddy * strain
                    src = produce - dissip
                else:
                    src = (
                        (prod_coeff * produce - dissip_coeff * dissip)
                        * dissip
                        / jnp.maximum(kinetic, turb_floor)
                    )
                if f == 3:
                    spread_by = heat_diffuse + eddy * (1.0 / 0.9)
                elif f == 5:
                    spread_by = molecular + eddy * (1.0 / 1.3)
                else:
                    spread_by = diffuse
                store(
                    f, plane, index, mid + time_step * (spread_by * laplace - transport + src)
                )
            return carry

        for plane in (1, 2):
            lax.fori_loop(0, fine_rows // ROW, functools.partial(chunk, plane), 0)

    def store_mid(f, plane, index, value):
        fields1[f, plane, pl.ds(pl.multiple_of(index * ROW + ROW, ROW), ROW), :] = value

    def store_last(f, plane, index, value):
        here = pl.ds(pl.multiple_of(index * ROW, ROW), ROW)
        if f < 3:
            vel_out[f, plane - 1, here, :] = value
        elif f == 3:
            temp_out[plane - 1, here, :] = value
        else:
            turb_out[f - 4, plane - 1, here, :] = value

    pack = win // SWEEPS

    def pack_potential():
        for z in range(0, depth, pack):
            to_left = jnp.zeros((rows, LANES), jnp.float32)
            to_right = to_left
            for k in range(pack):
                value = pot_a[z + k + 1]
                to_left = jnp.where(slot == k, left_roll(value, SWEEPS - SWEEPS * k), to_left)
                to_right = jnp.where(slot == k, left_roll(value, xl - SWEEPS * k), to_right)
            halo_out1[0, z // pack] = to_left
            halo_out1[1, z // pack] = to_right

    def framed(own, from_left, from_right, k):
        left = left_roll(from_left, SWEEPS * k)
        right = left_roll(from_right, SWEEPS * k - (win - SWEEPS))
        whole = jnp.where(
            inner < SWEEPS, left, jnp.where(inner >= win - SWEEPS, right, own)
        )
        return jnp.where(group < 3, whole, 0.0)

    for step in range(STEPS):
        if step == 0:
            for fetch in fetches:
                fetch.wait()
        restrict_and_window(step)
        if step == 0:
            pl.semaphore_wait(barrier, n - 1)
        forward = spread(step, send_f, recv_f, f_send_sem, f_recv_sem)
        for copy in forward:
            copy.start()
        if step == 0:
            halos = halo_copies(0)
            start_pair(halos)
        planes = plane_copies(step)
        start_pair(planes)
        recv_f[step, me] = send_f[step, me]
        if step == 0:
            pot_a[0] = jnp.zeros((rows, LANES), jnp.float32)
            pot_a[depth + 1] = jnp.zeros((rows, LANES), jnp.float32)
            pot_b[0] = jnp.zeros((rows, LANES), jnp.float32)
            pot_b[depth + 1] = jnp.zeros((rows, LANES), jnp.float32)
        receive_pair(halos)
        if step == 0:
            for z in range(depth):
                sides = halo_in0[0, z], halo_in0[1, z]
                pot_a[z + 1] = framed(own_ref[0, z], *sides, 0)
                one, two, three = turned(framed(own_ref[1, z], *sides, 1))
                field1[z] = jnp.where(group < 2, one, two)
                field2[z] = jnp.where(group == 0, two, three)
                coil[z] = framed(own_ref[2, z], *sides, 2)
        else:
            for z in range(depth):
                sides = halo_in1[0, z // pack], halo_in1[1, z // pack]
                pot_a[z + 1] = framed(pot_a[z + 1], *sides, z % pack)
        sent_pair(halos)
        for copy in forward:
            copy.wait_recv()
        relax_all(step)
        back = spread(step, send_b, recv_b, b_send_sem, b_recv_sem)
        for copy in back:
            copy.start()
        recv_b[step, me] = send_b[step, me]
        if step == 0:
            pack_potential()
            halos = halo_copies(1)
            start_pair(halos)
        else:
            for c in range(3):
                for z in range(depth):
                    at = c * win + SWEEPS
                    pot_out[c, z] = pot_a[z + 1][:, at : at + xl]
        for copy in forward:
            copy.wait_send()
        for copy in back:
            copy.wait_recv()
        prolong_loads(step)
        receive_pair(planes)
        advance_all(step, store_mid if step == 0 else store_last)
        for copy in back:
            copy.wait_send()
        sent_pair(planes)


def fused_on_device(
    melt_speeds,
    heat_state,
    eddy_quantities,
    zone_labels,
    zone_resistivity_inverse,
    imposed_induction,
    winding_current,
    window_entry_induction_guess,
):
    n = lax.axis_size("slab")
    _, xl, rows, depth = imposed_induction.shape
    _, fine_rows, width = heat_state.shape
    win = xl + 2 * SWEEPS
    coarse = [
        jnp.transpose(value, (0, 3, 2, 1))
        for value in (window_entry_induction_guess, imposed_induction, winding_current)
    ]

    def vmem(*shape):
        return pltpu.VMEM(shape, jnp.float32)

    plane = (depth, rows, LANES)
    dma = pltpu.SemaphoreType.DMA
    whole = pl.BlockSpec(memory_space=pltpu.VMEM)
    anywhere = pl.BlockSpec(memory_space=pl.ANY)
    vel, temp, turb, pot = pl.pallas_call(
        functools.partial(fused_kernel, n, xl),
        out_shape=(
            jax.ShapeDtypeStruct(melt_speeds.shape, jnp.float32),
            jax.ShapeDtypeStruct(heat_state.shape, jnp.float32),
            jax.ShapeDtypeStruct(eddy_quantities.shape, jnp.float32),
            jax.ShapeDtypeStruct((3, depth, rows, xl), jnp.float32),
        ),
        in_specs=[
            anywhere,
            anywhere,
            anywhere,
            whole,
            pl.BlockSpec(memory_space=pltpu.SMEM),
            whole,
            whole,
            whole,
        ],
        out_specs=(whole,) * 4,
        scratch_shapes=[
            vmem(6, 4, fine_rows + 2 * ROW, width),
            vmem(6, 4, fine_rows + 2 * ROW, width),
            vmem(STEPS, n, rows, LANES),
            vmem(STEPS, n, rows, LANES),
            vmem(STEPS, n, rows // 2, LANES),
            vmem(STEPS, n, rows // 2, LANES),
            vmem(3, *plane),
            vmem(2, *plane),
            vmem(2, *plane),
            vmem(2, depth * SWEEPS // win, rows, LANES),
            vmem(2, depth * SWEEPS // win, rows, LANES),
            vmem(depth + 2, rows, LANES),
            vmem(depth + 2, rows, LANES),
            vmem(*plane),
            vmem(*plane),
            vmem(*plane),
            vmem(*plane),
            vmem(*plane),
            vmem(*plane),
            vmem(4 * fine_rows, width),
            vmem(rows, width // 2),
            dma((3,)),
            dma((STEPS, n)),
            dma((STEPS, n)),
            dma((STEPS, n)),
            dma((STEPS, n)),
            dma((STEPS, 2)),
            dma((STEPS, 2)),
            dma((STEPS, 2)),
            dma((STEPS, 2)),
        ],
        compiler_params=pltpu.CompilerParams(
            collective_id=0, has_side_effects=True, vmem_limit_bytes=40 * 1024 * 1024
        ),
    )(melt_speeds, heat_state, eddy_quantities, zone_labels, zone_resistivity_inverse, *coarse)
    return vel, temp, turb, jnp.transpose(pot, (0, 3, 2, 1))


def fits_fused(n, heat_state, imposed_induction):
    _, xl, rows, depth = imposed_induction.shape
    planes, fine_rows, width = heat_state.shape
    win = xl + 2 * SWEEPS
    return (
        STEPS == 2
        and SWEEPS % 2 == 0
        and n > 1
        and planes == 2
        and depth == n
        and rows == 2 * ROW
        and fine_rows == 2 * rows
        and width == 2 * n * xl
        and width % (4 * LANES) == 0
        and 4 * win == LANES
        and xl == 2 * SWEEPS
        and n % (LANES // xl) == 0
        and depth % (win // SWEEPS) == 0
    )


def on_device(*args):
    if fits_fused(lax.axis_size("slab"), args[1], args[5]):
        return fused_on_device(*args)
    return layered_on_device(*args)


def solution(mesh):
    return jax.shard_map(
        on_device,
        mesh=mesh,
        in_specs=(
            P(None, ("groups", "slab"), None, None),
            P(("groups", "slab"), None, None),
            P(None, ("groups", "slab"), None, None),
            P(("groups", "slab"), None, None),
            P(),
            P(None, ("groups", "slab"), None, None),
            P(None, ("groups", "slab"), None, None),
            P(None, ("groups", "slab"), None, None),
        ),
        out_specs=(
            P(None, ("groups", "slab"), None, None),
            P(("groups", "slab"), None, None),
            P(None, ("groups", "slab"), None, None),
            P(None, ("groups", "slab"), None, None),
        ),
        check_vma=False,
    )
```

```python
import functools

import jax
import jax.numpy as jnp
from jax import lax
from jax.experimental import pallas as pl
from jax.experimental.pallas import tpu as pltpu
from jax.sharding import PartitionSpec as P

STEPS = 2
SWEEPS = 8


time_step = 0.02
molecular = 0.01
heat_diffuse = 0.01
eddy_coeff = 0.09
prod_coeff = 1.44
dissip_coeff = 1.92
turb_floor = 0.05
coupling = 1.0
thermal_gradient_factor = 0.3


def extended(block, sides, width):
    for axis, dim in sides:
        count = lax.axis_size(axis)
        forward = [(i, i + 1) for i in range(count - 1)]
        backward = [(target, source) for source, target in forward]
        low = lax.ppermute(
            lax.slice_in_dim(block, block.shape[dim] - width, None, axis=dim), axis, forward
        )
        high = lax.ppermute(lax.slice_in_dim(block, 0, width, axis=dim), axis, backward)
        block = jnp.concatenate([low, block, high], axis=dim)
    return block


def reduce_onto_parent(block):
    comps, depth, rows, cols = block.shape
    shaped = block.reshape(comps, depth // 2, 2, rows // 2, 2, cols // 2, 2)
    return jnp.mean(shaped, axis=(2, 4, 6))


def prolong(block):
    comps, depth, rows, cols = block.shape
    wide = jnp.broadcast_to(
        block[:, :, None, :, None, :, None], (comps, depth, 2, rows, 2, cols, 2)
    )
    return wide.reshape(comps, depth * 2, rows * 2, cols * 2)


def cross(left_vec, right_vec):
    return jnp.stack(
        [
            left_vec[1] * right_vec[2] - left_vec[2] * right_vec[1],
            left_vec[2] * right_vec[0] - left_vec[0] * right_vec[2],
            left_vec[0] * right_vec[1] - left_vec[1] * right_vec[0],
        ],
        0,
    )


def neighbours(padded):
    return (
        padded[:, 2:, 1:-1, 1:-1]
        + padded[:, :-2, 1:-1, 1:-1]
        + padded[:, 1:-1, 2:, 1:-1]
        + padded[:, 1:-1, :-2, 1:-1]
        + padded[:, 1:-1, 1:-1, 2:]
        + padded[:, 1:-1, 1:-1, :-2]
    )


def ohmic_admittance(zone_labels, zone_resistivity_inverse, heat_state):
    labels = jnp.arange(zone_resistivity_inverse.shape[0], dtype=jnp.int32)
    onehot = zone_labels[None] == labels[:, None, None, None]
    searched_higher = jnp.sum(
        jnp.where(onehot, zone_resistivity_inverse[:, None, None, None], jnp.float32(0.0)), axis=0
    )
    return (
        searched_higher
        * reduce_onto_parent(jnp.exp(-thermal_gradient_factor * heat_state)[None])[0]
    )


def faces(potential):
    padded = extended(potential, (("slab", 1),), 1)
    return jnp.pad(padded, ((0, 0), (0, 0), (1, 1), (1, 1)))


def relax(coupled, imposed_induction, winding_current, potential):
    conduct = coupled[3]
    motional = cross(coupled[:3], imposed_induction)
    source = conduct * motional + winding_current
    diagonal = 6.0 + coupling * conduct
    for sweep_index in range(SWEEPS):
        potential = (source + neighbours(faces(potential))) / diagonal
    drive_field = motional - coupling * potential
    current = conduct * drive_field + winding_current
    lorentz = cross(current, imposed_induction)
    joule = conduct * jnp.sum(drive_field * drive_field, axis=0)
    return (potential, jnp.concatenate([lorentz, joule[None]], 0))


def advance(padded, lorentz, joule):
    bordered = jnp.pad(padded, ((0, 0), (0, 0), (0, 0), (1, 1)))
    center = bordered[:, 1:-1, 1:-1, 1:-1]
    z_plus = bordered[:, 2:, 1:-1, 1:-1]
    z_minus = bordered[:, :-2, 1:-1, 1:-1]
    y_plus = bordered[:, 1:-1, 2:, 1:-1]
    y_minus = bordered[:, 1:-1, :-2, 1:-1]
    x_plus = bordered[:, 1:-1, 1:-1, 2:]
    x_minus = bordered[:, 1:-1, 1:-1, :-2]
    grad_z = 0.5 * (z_plus - z_minus)
    grad_y = 0.5 * (y_plus - y_minus)
    grad_x = 0.5 * (x_plus - x_minus)
    laplace = z_plus + z_minus + y_plus + y_minus + x_plus + x_minus - 6.0 * center
    kinetic = center[4]
    dissip = center[5]
    transport = center[0] * grad_x + center[1] * grad_y + center[2] * grad_z
    eddy_visc = eddy_coeff * kinetic * kinetic / jnp.maximum(dissip, turb_floor)
    strain = jnp.sum(
        grad_x[:3] * grad_x[:3] + grad_y[:3] * grad_y[:3] + grad_z[:3] * grad_z[:3], axis=0
    )
    produce = eddy_visc * strain
    diffuse = jnp.stack(
        [
            molecular + eddy_visc,
            molecular + eddy_visc,
            molecular + eddy_visc,
            heat_diffuse + eddy_visc / 0.9,
            molecular + eddy_visc,
            molecular + eddy_visc / 1.3,
        ],
        0,
    )
    dissip_source = (
        (prod_coeff * produce - dissip_coeff * dissip) * dissip / jnp.maximum(kinetic, turb_floor)
    )
    source = jnp.concatenate(
        [lorentz, joule[None], (produce - dissip)[None], dissip_source[None]], 0
    )
    return center + time_step * (diffuse * laplace - transport + source)


def flow_step(induction_tables, em_loads):
    padded = extended(induction_tables, (("slab", 1),), 1)
    padded = jnp.pad(padded, ((0, 0), (0, 0), (1, 1), (0, 0)))
    return advance(padded, em_loads[:3], em_loads[3])


def local_coupled(induction_tables, zone_labels, zone_resistivity_inverse):
    conduct = ohmic_admittance(zone_labels, zone_resistivity_inverse, induction_tables[3])
    return jnp.concatenate([reduce_onto_parent(induction_tables[:3]), conduct[None]], 0)


def layered_on_device(
    melt_speeds,
    heat_state,
    eddy_quantities,
    zone_labels,
    zone_resistivity_inverse,
    imposed_induction,
    winding_current,
    window_entry_induction_guess,
):
    induction_tables = jnp.concatenate([melt_speeds, heat_state[None], eddy_quantities], 0)
    arrived = (
        lax.all_to_all(
            window_entry_induction_guess, "slab", split_axis=3, concat_axis=1, tiled=True
        ),
        lax.all_to_all(imposed_induction, "slab", split_axis=3, concat_axis=1, tiled=True),
        lax.all_to_all(winding_current, "slab", split_axis=3, concat_axis=1, tiled=True),
    )
    potential = jnp.transpose(arrived[0], (0, 3, 2, 1))
    field_local = jnp.transpose(arrived[1], (0, 3, 2, 1))
    coil_local = jnp.transpose(arrived[2], (0, 3, 2, 1))
    for step_index in range(STEPS):
        coupled = local_coupled(induction_tables, zone_labels, zone_resistivity_inverse)
        potential, em_loads = relax(coupled, field_local, coil_local, potential)
        induction_tables = flow_step(induction_tables, prolong(em_loads))
    potential = lax.all_to_all(
        jnp.transpose(potential, (0, 3, 2, 1)), "slab", split_axis=1, concat_axis=3, tiled=True
    )
    return (induction_tables[:3], induction_tables[3], induction_tables[4:], potential)


ROW = 8
LANES = 128
MESH = pl.DeviceIdType.MESH


def iota(shape, dim):
    return lax.broadcasted_iota(jnp.int32, shape, dim)


def thirds(value):
    high = value.astype(jnp.bfloat16)
    rest = value - high.astype(jnp.float32)
    middle = rest.astype(jnp.bfloat16)
    low = (rest - middle.astype(jnp.float32)).astype(jnp.bfloat16)
    return high, middle, low


def times_right(value, matrix):
    rows = value.shape[0]
    out = jnp.dot(
        jnp.concatenate(thirds(value), 0), matrix, preferred_element_type=jnp.float32
    )
    return out[:rows] + out[rows : 2 * rows] + out[2 * rows :]


def times_left(matrix, value):
    return jnp.dot(
        jnp.concatenate([matrix] * 3, 1),
        jnp.concatenate(thirds(value), 0),
        preferred_element_type=jnp.float32,
    )


def pairing(shape, fine_dim, scale):
    fine = lax.shift_right_logical(iota(shape, fine_dim), 1)
    return jnp.where(fine == iota(shape, 1 - fine_dim), scale, 0.0).astype(jnp.bfloat16)


def left_roll(value, shift):
    width = value.shape[-1]
    shift = shift % width
    return value if shift == 0 else pltpu.roll(value, width - shift, value.ndim - 1)


def fused_kernel(
    n,
    xl,
    melt_ref,
    heat_ref,
    eddy_ref,
    zone_ref,
    table_ref,
    guess_ref,
    induction_ref,
    winding_ref,
    vel_out,
    temp_out,
    turb_out,
    pot_out,
    fields0,
    fields1,
    send_f,
    recv_f,
    send_b,
    recv_b,
    own_ref,
    halo_out0,
    halo_in0,
    halo_out1,
    halo_in1,
    pot_a,
    pot_b,
    field1,
    field2,
    coil,
    emf,
    source,
    inverse,
    loads,
    zone_sigma,
    load_sem,
    f_send_sem,
    f_recv_sem,
    b_send_sem,
    b_recv_sem,
    p_send_sem,
    p_recv_sem,
    h_send_sem,
    h_recv_sem,
):
    me = lax.axis_index("slab")
    fields = (fields0, fields1)
    halo_out = (halo_out0, halo_out1)
    halo_in = (halo_in0, halo_in1)
    win = xl + 2 * SWEEPS
    depth, rows = guess_ref.shape[1:3]
    fine_rows, width = heat_ref.shape[1:]
    body = pl.ds(ROW, fine_rows)
    cols = width // 2
    lane = iota((rows, LANES), 1)
    group = lane // win
    inner = lane % win
    sub = iota((rows, LANES), 0)

    def peer(index):
        return {"slab": index}

    fetches = [
        pltpu.make_async_copy(melt_ref, fields0.at[0:3, 1:3, body, :], load_sem.at[0]),
        pltpu.make_async_copy(heat_ref, fields0.at[3, 1:3, body, :], load_sem.at[1]),
        pltpu.make_async_copy(eddy_ref, fields0.at[4:6, 1:3, body, :], load_sem.at[2]),
    ]
    for fetch in fetches:
        fetch.start()

    barrier = pltpu.get_barrier_semaphore()
    for offset in range(1, n):
        pl.semaphore_signal(
            barrier, inc=1, device_id=peer(lax.rem(me + offset, n)), device_id_type=MESH
        )

    for block in fields:
        edge = jnp.zeros((6, 4, ROW, width), jnp.float32)
        block[:, :, 0:ROW, :] = edge
        block[:, :, ROW + fine_rows :, :] = edge

    @pl.when(me == 0)
    def _():
        for block in fields:
            block[:, 0, body, :] = jnp.zeros((6, fine_rows, width), jnp.float32)
        for block in halo_in:
            block[0] = jnp.zeros(block.shape[1:], jnp.float32)

    @pl.when(me == n - 1)
    def _():
        for block in fields:
            block[:, 3, body, :] = jnp.zeros((6, fine_rows, width), jnp.float32)
        for block in halo_in:
            block[1] = jnp.zeros(block.shape[1:], jnp.float32)

    labels = zone_ref[0]
    sigma0 = jnp.zeros(labels.shape, jnp.float32)
    for region in range(table_ref.shape[0]):
        sigma0 = sigma0 + jnp.where(labels == region, table_ref[region], 0.0)
    zone_sigma[...] = sigma0

    def blank(lanes):
        return jnp.zeros((rows, lanes), jnp.float32)

    for a, coarse_ref in enumerate((guess_ref, induction_ref, winding_ref)):
        for z in range(depth):
            own_ref[a, z] = jnp.concatenate(
                [
                    blank(SWEEPS),
                    coarse_ref[0, z],
                    blank(2 * SWEEPS),
                    coarse_ref[1, z],
                    blank(2 * SWEEPS),
                    coarse_ref[2, z],
                    blank(SWEEPS + win),
                ],
                1,
            )

    slot = inner // SWEEPS
    for z in range(depth):
        to_left = jnp.zeros((rows, LANES), jnp.float32)
        to_right = to_left
        for a in range(3):
            value = own_ref[a, z]
            to_left = jnp.where(slot == a, left_roll(value, SWEEPS - SWEEPS * a), to_left)
            to_right = jnp.where(slot == a, left_roll(value, xl - SWEEPS * a), to_right)
        halo_out0[0, z] = to_left
        halo_out0[1, z] = to_right

    def plane_copies(step):
        block = fields[step]
        down = pltpu.make_async_remote_copy(
            src_ref=block.at[:, 1, body, :],
            dst_ref=block.at[:, 3, body, :],
            send_sem=p_send_sem.at[step, 0],
            recv_sem=p_recv_sem.at[step, 0],
            device_id=peer(me - 1),
            device_id_type=MESH,
        )
        up = pltpu.make_async_remote_copy(
            src_ref=block.at[:, 2, body, :],
            dst_ref=block.at[:, 0, body, :],
            send_sem=p_send_sem.at[step, 1],
            recv_sem=p_recv_sem.at[step, 1],
            device_id=peer(me + 1),
            device_id_type=MESH,
        )
        return down, up

    def halo_copies(step):
        down = pltpu.make_async_remote_copy(
            src_ref=halo_out[step].at[0],
            dst_ref=halo_in[step].at[1],
            send_sem=h_send_sem.at[step, 0],
            recv_sem=h_recv_sem.at[step, 0],
            device_id=peer(me - 1),
            device_id_type=MESH,
        )
        up = pltpu.make_async_remote_copy(
            src_ref=halo_out[step].at[1],
            dst_ref=halo_in[step].at[0],
            send_sem=h_send_sem.at[step, 1],
            recv_sem=h_recv_sem.at[step, 1],
            device_id=peer(me + 1),
            device_id_type=MESH,
        )
        return down, up

    def start_down(pair):
        @pl.when(me > 0)
        def _():
            pair[0].start()

    def start_up(pair):
        @pl.when(me < n - 1)
        def _():
            pair[1].start()

    def start_pair(pair):
        start_down(pair)
        start_up(pair)

    def receive_pair(pair):
        @pl.when(me < n - 1)
        def _():
            pair[0].wait_recv()

        @pl.when(me > 0)
        def _():
            pair[1].wait_recv()

    def sent_pair(pair):
        @pl.when(me > 0)
        def _():
            pair[0].wait_send()

        @pl.when(me < n - 1)
        def _():
            pair[1].wait_send()

    def spread(step, send, recv, send_sem, recv_sem):
        copies = []
        for offset in sorted(range(1, n), key=lambda o: abs(2 * o - n)):
            target = lax.rem(me + offset, n)
            copies.append(
                pltpu.make_async_remote_copy(
                    src_ref=send.at[step, target],
                    dst_ref=recv.at[step, me],
                    send_sem=send_sem.at[step, offset],
                    recv_sem=recv_sem.at[step, offset],
                    device_id=peer(target),
                    device_id_type=MESH,
                )
            )
        return copies

    halve_rows = pairing((4 * rows, 4 * fine_rows), 1, 0.125)
    halve_cols = pairing((2 * LANES, LANES), 0, 1.0)
    double_rows = pairing((4 * fine_rows, 4 * rows), 0, 1.0)
    double_cols = pairing((LANES, 2 * LANES), 1, 1.0)

    def restrict_and_window(step):
        block = fields[step]
        parts = [block[f, 1, body, :] + block[f, 2, body, :] for f in range(3)]
        parts.append(
            jnp.exp(-thermal_gradient_factor * block[3, 1, body, :])
            + jnp.exp(-thermal_gradient_factor * block[3, 2, body, :])
        )
        short = times_left(halve_rows, jnp.concatenate(parts, 0))
        coarse = jnp.concatenate(
            [
                times_right(short[:, at : at + 2 * LANES], halve_cols)
                for at in range(0, width, 2 * LANES)
            ],
            1,
        )
        comps = [coarse[c * rows : (c + 1) * rows] for c in range(4)]
        comps[3] = comps[3] * zone_sigma[...]
        for target in range(n):
            first = target * xl - SWEEPS
            message = jnp.zeros((rows, LANES), jnp.float32)
            for c in range(4):
                moved = left_roll(comps[c], first - c * win)[:, :LANES]
                message = jnp.where(group == c, moved, message)
            send_f[step, target] = message

    def turned(value):
        return left_roll(value, win), left_roll(value, 2 * win), left_roll(value, 3 * win)

    def relax_all(step):
        x_at = me * xl - SWEEPS + inner
        valid = (x_at >= 0) & (x_at < cols) & (group < 3)

        def prepare(z):
            value = recv_f[step, z]
            one, two, three = turned(value)
            next_comp = jnp.where(group < 2, one, two)
            last_comp = jnp.where(group == 0, two, three)
            sigma = jnp.where(group == 0, three, jnp.where(group == 1, two, one))
            motional = next_comp * field2[z] - last_comp * field1[z]
            emf[z] = motional
            source[z] = sigma * motional + coil[z]
            inverse[z] = jnp.where(valid, 1.0 / (6.0 + coupling * sigma), 0.0)

        for z in range(depth):
            prepare(z)

        def sweep(old, new):
            for z in range(depth):
                centre = old[z + 1]
                total = source[z] + old[z] + old[z + 2]
                total = total + left_roll(centre, 1) + left_roll(centre, LANES - 1)
                total = total + jnp.where(sub == 0, 0.0, pltpu.roll(centre, 1, 0))
                total = total + jnp.where(sub == rows - 1, 0.0, pltpu.roll(centre, rows - 1, 0))
                new[z + 1] = total * inverse[z]

        def two_sweeps(index, carry):
            sweep(pot_a, pot_b)
            sweep(pot_b, pot_a)
            return carry

        lax.fori_loop(0, SWEEPS // 2, two_sweeps, 0)

        half = rows // 2
        packed = iota((half, LANES), 1) // xl

        def load(z):
            value = recv_f[step, z]
            one, two, three = turned(value)
            sigma = jnp.where(group == 0, three, jnp.where(group == 1, two, one))
            drive = emf[z] - coupling * pot_a[z + 1]
            current = sigma * drive + coil[z]
            one, two, three = turned(current)
            next_comp = jnp.where(group < 2, one, two)
            last_comp = jnp.where(group == 0, two, three)
            force = next_comp * field2[z] - last_comp * field1[z]
            one, two, three = turned(drive * drive)
            both = jnp.where(group == 3, value * (one + two + three), force)
            message = jnp.zeros((half, LANES), jnp.float32)
            for h in range(2):
                piece = both[h * half : (h + 1) * half]
                for c in range(4):
                    at = 4 * h + c
                    moved = left_roll(piece, c * win + SWEEPS - at * xl)
                    message = jnp.where(packed == at, moved, message)
            send_b[step, z] = message

        for z in range(depth):
            load(z)

    def prolong_loads(step):
        half = rows // 2
        packed = iota((half, LANES), 1) // xl
        per = LANES // xl
        strips = []
        for c in range(4):
            for h in range(2):
                strip = []
                for first in range(0, n, per):
                    piece = jnp.zeros((half, LANES), jnp.float32)
                    for d in range(per):
                        moved = left_roll(recv_b[step, first + d], (4 * h + c - d) * xl)
                        piece = jnp.where(packed == d, moved, piece)
                    strip.append(piece)
                strips.append(jnp.concatenate(strip, 1))
        coarse = jnp.concatenate(strips, 0)
        wide = jnp.concatenate(
            [
                times_right(coarse[:, at : at + LANES], double_cols)
                for at in range(0, cols, LANES)
            ],
            1,
        )
        loads[...] = times_left(double_rows, wide)

    def advance_plane(step, plane, store):
        block = fields[step]
        sub8 = iota((ROW, width), 0)
        lane8 = iota((ROW, width), 1)

        def chunk(index):
            low = index * ROW
            at = low + ROW
            high = at + ROW
            here = pl.ds(at, ROW)
            centre = [block[f, plane, here, :] for f in range(6)]
            kinetic, dissip = centre[4], centre[5]
            eddy = eddy_coeff * kinetic * kinetic / jnp.maximum(dissip, turb_floor)
            diffuse = molecular + eddy
            strain = None
            for f in range(6):
                mid = centre[f]
                z_minus = block[f, plane - 1, here, :]
                z_plus = block[f, plane + 1, here, :]
                before = block[f, plane, pl.ds(low, ROW), :]
                after = block[f, plane, pl.ds(high, ROW), :]
                y_minus = pltpu.roll(jnp.where(sub8 == ROW - 1, before, mid), 1, 0)
                y_plus = pltpu.roll(jnp.where(sub8 == 0, after, mid), ROW - 1, 0)
                x_minus = jnp.where(lane8 == 0, 0.0, pltpu.roll(mid, 1, 1))
                x_plus = jnp.where(lane8 == width - 1, 0.0, pltpu.roll(mid, width - 1, 1))
                laplace = (
                    (z_plus + z_minus) + (y_plus + y_minus) + (x_plus + x_minus) - 6.0 * mid
                )
                grad_z = 0.5 * (z_plus - z_minus)
                grad_y = 0.5 * (y_plus - y_minus)
                grad_x = 0.5 * (x_plus - x_minus)
                transport = centre[0] * grad_x + centre[1] * grad_y + centre[2] * grad_z
                if f < 3:
                    square = grad_x * grad_x + grad_y * grad_y + grad_z * grad_z
                    strain = square if strain is None else strain + square
                if f < 4:
                    src = loads[pl.ds(f * fine_rows + index * ROW, ROW), :]
                elif f == 4:
                    produce = eddy * strain
                    src = produce - dissip
                else:
                    src = (
                        (prod_coeff * produce - dissip_coeff * dissip)
                        * dissip
                        / jnp.maximum(kinetic, turb_floor)
                    )
                if f == 3:
                    spread_by = heat_diffuse + eddy * (1.0 / 0.9)
                elif f == 5:
                    spread_by = molecular + eddy * (1.0 / 1.3)
                else:
                    spread_by = diffuse
                store(
                    f, plane, index, mid + time_step * (spread_by * laplace - transport + src)
                )

        for index in range(fine_rows // ROW):
            chunk(index)

    def store_mid(f, plane, index, value):
        fields1[f, plane, pl.ds(index * ROW + ROW, ROW), :] = value

    def store_last(f, plane, index, value):
        here = pl.ds(index * ROW, ROW)
        if f < 3:
            vel_out[f, plane - 1, here, :] = value
        elif f == 3:
            temp_out[plane - 1, here, :] = value
        else:
            turb_out[f - 4, plane - 1, here, :] = value

    pack = win // SWEEPS

    def pack_potential():
        for z in range(0, depth, pack):
            to_left = jnp.zeros((rows, LANES), jnp.float32)
            to_right = to_left
            for k in range(pack):
                value = pot_a[z + k + 1]
                to_left = jnp.where(slot == k, left_roll(value, SWEEPS - SWEEPS * k), to_left)
                to_right = jnp.where(slot == k, left_roll(value, xl - SWEEPS * k), to_right)
            halo_out1[0, z // pack] = to_left
            halo_out1[1, z // pack] = to_right

    def framed(own, from_left, from_right, k):
        left = left_roll(from_left, SWEEPS * k)
        right = left_roll(from_right, SWEEPS * k - (win - SWEEPS))
        whole = jnp.where(
            inner < SWEEPS, left, jnp.where(inner >= win - SWEEPS, right, own)
        )
        return jnp.where(group < 3, whole, 0.0)

    pl.semaphore_wait(barrier, n - 1)
    halos = halo_copies(0)
    start_pair(halos)
    for fetch in fetches:
        fetch.wait()
    for row in (0, depth + 1):
        pot_a[row] = blank(LANES)
        pot_b[row] = blank(LANES)
    planes = plane_copies(0)
    for step in range(STEPS):
        restrict_and_window(step)
        forward = spread(step, send_f, recv_f, f_send_sem, f_recv_sem)
        for copy in forward:
            copy.start()
        recv_f[step, me] = send_f[step, me]
        receive_pair(halos)
        if step == 0:
            for z in range(depth):
                sides = halo_in0[0, z], halo_in0[1, z]
                pot_a[z + 1] = framed(own_ref[0, z], *sides, 0)
                one, two, three = turned(framed(own_ref[1, z], *sides, 1))
                field1[z] = jnp.where(group < 2, one, two)
                field2[z] = jnp.where(group == 0, two, three)
                coil[z] = framed(own_ref[2, z], *sides, 2)
        else:
            for z in range(depth):
                sides = halo_in1[0, z // pack], halo_in1[1, z // pack]
                pot_a[z + 1] = framed(pot_a[z + 1], *sides, z % pack)
        for copy in forward:
            copy.wait_recv()
        if step == 0:
            start_down(planes)
        start_up(planes)
        relax_all(step)
        back = spread(step, send_b, recv_b, b_send_sem, b_recv_sem)
        for copy in back:
            copy.start()
        recv_b[step, me] = send_b[step, me]
        sent_pair(halos)
        if step == 0:
            pack_potential()
            halos = halo_copies(1)
            start_pair(halos)
        else:
            for c in range(3):
                for z in range(depth):
                    at = c * win + SWEEPS
                    pot_out[c, z] = pot_a[z + 1][:, at : at + xl]
        for copy in forward:
            copy.wait_send()
        for copy in back:
            copy.wait_recv()
        prolong_loads(step)
        receive_pair(planes)
        if step == 0:
            following = plane_copies(1)
            advance_plane(step, 1, store_mid)
            start_down(following)
            advance_plane(step, 2, store_mid)
        else:
            advance_plane(step, 1, store_last)
            advance_plane(step, 2, store_last)
        for copy in back:
            copy.wait_send()
        sent_pair(planes)
        planes = following


def fused_on_device(
    melt_speeds,
    heat_state,
    eddy_quantities,
    zone_labels,
    zone_resistivity_inverse,
    imposed_induction,
    winding_current,
    window_entry_induction_guess,
):
    n = lax.axis_size("slab")
    _, xl, rows, depth = imposed_induction.shape
    _, fine_rows, width = heat_state.shape
    win = xl + 2 * SWEEPS
    coarse = [
        jnp.transpose(value, (0, 3, 2, 1))
        for value in (window_entry_induction_guess, imposed_induction, winding_current)
    ]

    def vmem(*shape):
        return pltpu.VMEM(shape, jnp.float32)

    plane = (depth, rows, LANES)
    dma = pltpu.SemaphoreType.DMA
    whole = pl.BlockSpec(memory_space=pltpu.VMEM)
    anywhere = pl.BlockSpec(memory_space=pl.ANY)
    vel, temp, turb, pot = pl.pallas_call(
        functools.partial(fused_kernel, n, xl),
        out_shape=(
            jax.ShapeDtypeStruct(melt_speeds.shape, jnp.float32),
            jax.ShapeDtypeStruct(heat_state.shape, jnp.float32),
            jax.ShapeDtypeStruct(eddy_quantities.shape, jnp.float32),
            jax.ShapeDtypeStruct((3, depth, rows, xl), jnp.float32),
        ),
        in_specs=[
            anywhere,
            anywhere,
            anywhere,
            whole,
            pl.BlockSpec(memory_space=pltpu.SMEM),
            whole,
            whole,
            whole,
        ],
        out_specs=(whole,) * 4,
        scratch_shapes=[
            vmem(6, 4, fine_rows + 2 * ROW, width),
            vmem(6, 4, fine_rows + 2 * ROW, width),
            vmem(STEPS, n, rows, LANES),
            vmem(STEPS, n, rows, LANES),
            vmem(STEPS, n, rows // 2, LANES),
            vmem(STEPS, n, rows // 2, LANES),
            vmem(3, *plane),
            vmem(2, *plane),
            vmem(2, *plane),
            vmem(2, depth * SWEEPS // win, rows, LANES),
            vmem(2, depth * SWEEPS // win, rows, LANES),
            vmem(depth + 2, rows, LANES),
            vmem(depth + 2, rows, LANES),
            vmem(*plane),
            vmem(*plane),
            vmem(*plane),
            vmem(*plane),
            vmem(*plane),
            vmem(*plane),
            vmem(4 * fine_rows, width),
            vmem(rows, width // 2),
            dma((3,)),
            dma((STEPS, n)),
            dma((STEPS, n)),
            dma((STEPS, n)),
            dma((STEPS, n)),
            dma((STEPS, 2)),
            dma((STEPS, 2)),
            dma((STEPS, 2)),
            dma((STEPS, 2)),
        ],
        compiler_params=pltpu.CompilerParams(
            collective_id=0, has_side_effects=True, vmem_limit_bytes=40 * 1024 * 1024
        ),
    )(melt_speeds, heat_state, eddy_quantities, zone_labels, zone_resistivity_inverse, *coarse)
    return vel, temp, turb, jnp.transpose(pot, (0, 3, 2, 1))


def fits_fused(n, heat_state, imposed_induction):
    _, xl, rows, depth = imposed_induction.shape
    planes, fine_rows, width = heat_state.shape
    win = xl + 2 * SWEEPS
    return (
        STEPS == 2
        and SWEEPS % 2 == 0
        and n > 1
        and planes == 2
        and depth == n
        and rows == 2 * ROW
        and fine_rows == 2 * rows
        and width == 2 * n * xl
        and width % (4 * LANES) == 0
        and 4 * win == LANES
        and xl == 2 * SWEEPS
        and n % (LANES // xl) == 0
        and depth % (win // SWEEPS) == 0
    )


def on_device(*args):
    if fits_fused(lax.axis_size("slab"), args[1], args[5]):
        return fused_on_device(*args)
    return layered_on_device(*args)


def solution(mesh):
    return jax.shard_map(
        on_device,
        mesh=mesh,
        in_specs=(
            P(None, ("groups", "slab"), None, None),
            P(("groups", "slab"), None, None),
            P(None, ("groups", "slab"), None, None),
            P(("groups", "slab"), None, None),
            P(),
            P(None, ("groups", "slab"), None, None),
            P(None, ("groups", "slab"), None, None),
            P(None, ("groups", "slab"), None, None),
        ),
        out_specs=(
            P(None, ("groups", "slab"), None, None),
            P(("groups", "slab"), None, None),
            P(None, ("groups", "slab"), None, None),
            P(None, ("groups", "slab"), None, None),
        ),
        check_vma=False,
    )
```

```python
import functools

import jax
import jax.numpy as jnp
from jax import lax
from jax.experimental import pallas as pl
from jax.experimental.pallas import tpu as pltpu
from jax.sharding import PartitionSpec as P

STEPS = 2
SWEEPS = 8


time_step = 0.02
molecular = 0.01
heat_diffuse = 0.01
eddy_coeff = 0.09
prod_coeff = 1.44
dissip_coeff = 1.92
turb_floor = 0.05
coupling = 1.0
thermal_gradient_factor = 0.3


def extended(block, sides, width):
    for axis, dim in sides:
        count = lax.axis_size(axis)
        forward = [(i, i + 1) for i in range(count - 1)]
        backward = [(target, source) for source, target in forward]
        low = lax.ppermute(
            lax.slice_in_dim(block, block.shape[dim] - width, None, axis=dim), axis, forward
        )
        high = lax.ppermute(lax.slice_in_dim(block, 0, width, axis=dim), axis, backward)
        block = jnp.concatenate([low, block, high], axis=dim)
    return block


def reduce_onto_parent(block):
    comps, depth, rows, cols = block.shape
    shaped = block.reshape(comps, depth // 2, 2, rows // 2, 2, cols // 2, 2)
    return jnp.mean(shaped, axis=(2, 4, 6))


def prolong(block):
    comps, depth, rows, cols = block.shape
    wide = jnp.broadcast_to(
        block[:, :, None, :, None, :, None], (comps, depth, 2, rows, 2, cols, 2)
    )
    return wide.reshape(comps, depth * 2, rows * 2, cols * 2)


def cross(left_vec, right_vec):
    return jnp.stack(
        [
            left_vec[1] * right_vec[2] - left_vec[2] * right_vec[1],
            left_vec[2] * right_vec[0] - left_vec[0] * right_vec[2],
            left_vec[0] * right_vec[1] - left_vec[1] * right_vec[0],
        ],
        0,
    )


def neighbours(padded):
    return (
        padded[:, 2:, 1:-1, 1:-1]
        + padded[:, :-2, 1:-1, 1:-1]
        + padded[:, 1:-1, 2:, 1:-1]
        + padded[:, 1:-1, :-2, 1:-1]
        + padded[:, 1:-1, 1:-1, 2:]
        + padded[:, 1:-1, 1:-1, :-2]
    )


def ohmic_admittance(zone_labels, zone_resistivity_inverse, heat_state):
    labels = jnp.arange(zone_resistivity_inverse.shape[0], dtype=jnp.int32)
    onehot = zone_labels[None] == labels[:, None, None, None]
    searched_higher = jnp.sum(
        jnp.where(onehot, zone_resistivity_inverse[:, None, None, None], jnp.float32(0.0)), axis=0
    )
    return (
        searched_higher
        * reduce_onto_parent(jnp.exp(-thermal_gradient_factor * heat_state)[None])[0]
    )


def faces(potential):
    padded = extended(potential, (("slab", 1),), 1)
    return jnp.pad(padded, ((0, 0), (0, 0), (1, 1), (1, 1)))


def relax(coupled, imposed_induction, winding_current, potential):
    conduct = coupled[3]
    motional = cross(coupled[:3], imposed_induction)
    source = conduct * motional + winding_current
    diagonal = 6.0 + coupling * conduct
    for sweep_index in range(SWEEPS):
        potential = (source + neighbours(faces(potential))) / diagonal
    drive_field = motional - coupling * potential
    current = conduct * drive_field + winding_current
    lorentz = cross(current, imposed_induction)
    joule = conduct * jnp.sum(drive_field * drive_field, axis=0)
    return (potential, jnp.concatenate([lorentz, joule[None]], 0))


def advance(padded, lorentz, joule):
    bordered = jnp.pad(padded, ((0, 0), (0, 0), (0, 0), (1, 1)))
    center = bordered[:, 1:-1, 1:-1, 1:-1]
    z_plus = bordered[:, 2:, 1:-1, 1:-1]
    z_minus = bordered[:, :-2, 1:-1, 1:-1]
    y_plus = bordered[:, 1:-1, 2:, 1:-1]
    y_minus = bordered[:, 1:-1, :-2, 1:-1]
    x_plus = bordered[:, 1:-1, 1:-1, 2:]
    x_minus = bordered[:, 1:-1, 1:-1, :-2]
    grad_z = 0.5 * (z_plus - z_minus)
    grad_y = 0.5 * (y_plus - y_minus)
    grad_x = 0.5 * (x_plus - x_minus)
    laplace = z_plus + z_minus + y_plus + y_minus + x_plus + x_minus - 6.0 * center
    kinetic = center[4]
    dissip = center[5]
    transport = center[0] * grad_x + center[1] * grad_y + center[2] * grad_z
    eddy_visc = eddy_coeff * kinetic * kinetic / jnp.maximum(dissip, turb_floor)
    strain = jnp.sum(
        grad_x[:3] * grad_x[:3] + grad_y[:3] * grad_y[:3] + grad_z[:3] * grad_z[:3], axis=0
    )
    produce = eddy_visc * strain
    diffuse = jnp.stack(
        [
            molecular + eddy_visc,
            molecular + eddy_visc,
            molecular + eddy_visc,
            heat_diffuse + eddy_visc / 0.9,
            molecular + eddy_visc,
            molecular + eddy_visc / 1.3,
        ],
        0,
    )
    dissip_source = (
        (prod_coeff * produce - dissip_coeff * dissip) * dissip / jnp.maximum(kinetic, turb_floor)
    )
    source = jnp.concatenate(
        [lorentz, joule[None], (produce - dissip)[None], dissip_source[None]], 0
    )
    return center + time_step * (diffuse * laplace - transport + source)


def flow_step(induction_tables, em_loads):
    padded = extended(induction_tables, (("slab", 1),), 1)
    padded = jnp.pad(padded, ((0, 0), (0, 0), (1, 1), (0, 0)))
    return advance(padded, em_loads[:3], em_loads[3])


def local_coupled(induction_tables, zone_labels, zone_resistivity_inverse):
    conduct = ohmic_admittance(zone_labels, zone_resistivity_inverse, induction_tables[3])
    return jnp.concatenate([reduce_onto_parent(induction_tables[:3]), conduct[None]], 0)


def layered_on_device(
    melt_speeds,
    heat_state,
    eddy_quantities,
    zone_labels,
    zone_resistivity_inverse,
    imposed_induction,
    winding_current,
    window_entry_induction_guess,
):
    induction_tables = jnp.concatenate([melt_speeds, heat_state[None], eddy_quantities], 0)
    arrived = (
        lax.all_to_all(
            window_entry_induction_guess, "slab", split_axis=3, concat_axis=1, tiled=True
        ),
        lax.all_to_all(imposed_induction, "slab", split_axis=3, concat_axis=1, tiled=True),
        lax.all_to_all(winding_current, "slab", split_axis=3, concat_axis=1, tiled=True),
    )
    potential = jnp.transpose(arrived[0], (0, 3, 2, 1))
    field_local = jnp.transpose(arrived[1], (0, 3, 2, 1))
    coil_local = jnp.transpose(arrived[2], (0, 3, 2, 1))
    for step_index in range(STEPS):
        coupled = local_coupled(induction_tables, zone_labels, zone_resistivity_inverse)
        potential, em_loads = relax(coupled, field_local, coil_local, potential)
        induction_tables = flow_step(induction_tables, prolong(em_loads))
    potential = lax.all_to_all(
        jnp.transpose(potential, (0, 3, 2, 1)), "slab", split_axis=1, concat_axis=3, tiled=True
    )
    return (induction_tables[:3], induction_tables[3], induction_tables[4:], potential)


ROW = 8
LANES = 128
MESH = pl.DeviceIdType.MESH


def iota(shape, dim):
    return lax.broadcasted_iota(jnp.int32, shape, dim)


def thirds(value):
    high = value.astype(jnp.bfloat16)
    rest = value - high.astype(jnp.float32)
    middle = rest.astype(jnp.bfloat16)
    low = (rest - middle.astype(jnp.float32)).astype(jnp.bfloat16)
    return high, middle, low


def times_right(value, matrix):
    rows = value.shape[0]
    out = jnp.dot(
        jnp.concatenate(thirds(value), 0), matrix, preferred_element_type=jnp.float32
    )
    return out[:rows] + out[rows : 2 * rows] + out[2 * rows :]


def times_left(matrix, value):
    return jnp.dot(
        jnp.concatenate([matrix] * 3, 1),
        jnp.concatenate(thirds(value), 0),
        preferred_element_type=jnp.float32,
    )


def pairing(shape, fine_dim, scale):
    fine = lax.shift_right_logical(iota(shape, fine_dim), 1)
    return jnp.where(fine == iota(shape, 1 - fine_dim), scale, 0.0).astype(jnp.bfloat16)


def left_roll(value, shift):
    width = value.shape[-1]
    shift = shift % width
    return value if shift == 0 else pltpu.roll(value, width - shift, value.ndim - 1)


def fused_kernel(
    n,
    xl,
    melt_ref,
    heat_ref,
    eddy_ref,
    zone_ref,
    table_ref,
    guess_ref,
    induction_ref,
    winding_ref,
    vel_out,
    temp_out,
    turb_out,
    pot_out,
    fields0,
    fields1,
    send_f,
    recv_f,
    send_b,
    recv_b,
    own_ref,
    halo_out0,
    halo_in0,
    halo_out1,
    halo_in1,
    pot_a,
    pot_b,
    field1,
    field2,
    coil,
    emf,
    source,
    inverse,
    loads,
    zone_sigma,
    load_sem,
    f_send_sem,
    f_recv_sem,
    b_send_sem,
    b_recv_sem,
    p_send_sem,
    p_recv_sem,
    h_send_sem,
    h_recv_sem,
):
    me = lax.axis_index("slab")
    fields = (fields0, fields1)
    halo_out = (halo_out0, halo_out1)
    halo_in = (halo_in0, halo_in1)
    win = xl + 2 * SWEEPS
    depth, rows = guess_ref.shape[1:3]
    fine_rows, width = heat_ref.shape[1:]
    body = pl.ds(ROW, fine_rows)
    cols = width // 2
    lane = iota((rows, LANES), 1)
    group = lane // win
    inner = lane % win
    sub = iota((rows, LANES), 0)

    def peer(index):
        return {"slab": index}

    fetches = [
        pltpu.make_async_copy(melt_ref, fields0.at[0:3, 1:3, body, :], load_sem.at[0]),
        pltpu.make_async_copy(heat_ref, fields0.at[3, 1:3, body, :], load_sem.at[1]),
        pltpu.make_async_copy(eddy_ref, fields0.at[4:6, 1:3, body, :], load_sem.at[2]),
    ]
    for fetch in fetches:
        fetch.start()

    barrier = pltpu.get_barrier_semaphore()
    for offset in range(1, n):
        pl.semaphore_signal(
            barrier, inc=1, device_id=peer(lax.rem(me + offset, n)), device_id_type=MESH
        )

    for block in fields:
        edge = jnp.zeros((6, 4, ROW, width), jnp.float32)
        block[:, :, 0:ROW, :] = edge
        block[:, :, ROW + fine_rows :, :] = edge

    @pl.when(me == 0)
    def _():
        for block in fields:
            block[:, 0, body, :] = jnp.zeros((6, fine_rows, width), jnp.float32)
        for block in halo_in:
            block[0] = jnp.zeros(block.shape[1:], jnp.float32)

    @pl.when(me == n - 1)
    def _():
        for block in fields:
            block[:, 3, body, :] = jnp.zeros((6, fine_rows, width), jnp.float32)
        for block in halo_in:
            block[1] = jnp.zeros(block.shape[1:], jnp.float32)

    labels = zone_ref[0]
    sigma0 = jnp.zeros(labels.shape, jnp.float32)
    for region in range(table_ref.shape[0]):
        sigma0 = sigma0 + jnp.where(labels == region, table_ref[region], 0.0)
    zone_sigma[...] = sigma0

    def blank(lanes):
        return jnp.zeros((rows, lanes), jnp.float32)

    for a, coarse_ref in enumerate((guess_ref, induction_ref, winding_ref)):
        for z in range(depth):
            own_ref[a, z] = jnp.concatenate(
                [
                    blank(SWEEPS),
                    coarse_ref[0, z],
                    blank(2 * SWEEPS),
                    coarse_ref[1, z],
                    blank(2 * SWEEPS),
                    coarse_ref[2, z],
                    blank(SWEEPS + win),
                ],
                1,
            )

    slot = inner // SWEEPS
    pack = win // SWEEPS

    def pack_halos(out, values):
        for first in range(0, len(values), pack):
            to_left = blank(LANES)
            to_right = blank(LANES)
            for k in range(pack):
                value = values[first + k]()
                to_left = jnp.where(slot == k, left_roll(value, SWEEPS - SWEEPS * k), to_left)
                to_right = jnp.where(slot == k, left_roll(value, xl - SWEEPS * k), to_right)
            out[0, first // pack] = to_left
            out[1, first // pack] = to_right

    pack_halos(
        halo_out0,
        [functools.partial(own_ref.__getitem__, (a, z)) for z in range(depth) for a in range(3)],
    )

    def face_copy(source, step, field, here, part, down):
        side = 0 if down else 1
        return pltpu.make_async_remote_copy(
            src_ref=source,
            dst_ref=fields[step].at[field, 3 if down else 0, here, :],
            send_sem=p_send_sem.at[step, side, part],
            recv_sem=p_recv_sem.at[step, side, part],
            device_id=peer(me - 1 if down else me + 1),
            device_id_type=MESH,
        )

    def first_faces(down):
        at = 0 if down else 1
        return [
            face_copy(melt_ref.at[:, at], 0, slice(0, 3), body, 0, down),
            face_copy(heat_ref.at[at], 0, 3, body, 1, down),
            face_copy(eddy_ref.at[:, at], 0, slice(4, 6), body, 2, down),
        ]

    def later_faces(down):
        copies = []
        for part in range(fine_rows // ROW):
            here = pl.ds(ROW + part * ROW, ROW)
            mine = fields1.at[:, 1 if down else 2, here, :]
            copies.append(face_copy(mine, 1, slice(0, 6), here, part, down))
        return copies

    def halo_copies(step):
        down = pltpu.make_async_remote_copy(
            src_ref=halo_out[step].at[0],
            dst_ref=halo_in[step].at[1],
            send_sem=h_send_sem.at[step, 0],
            recv_sem=h_recv_sem.at[step, 0],
            device_id=peer(me - 1),
            device_id_type=MESH,
        )
        up = pltpu.make_async_remote_copy(
            src_ref=halo_out[step].at[1],
            dst_ref=halo_in[step].at[0],
            send_sem=h_send_sem.at[step, 1],
            recv_sem=h_recv_sem.at[step, 1],
            device_id=peer(me + 1),
            device_id_type=MESH,
        )
        return [down], [up]

    def start_down(copies):
        @pl.when(me > 0)
        def _():
            for copy in copies:
                copy.start()

    def start_up(copies):
        @pl.when(me < n - 1)
        def _():
            for copy in copies:
                copy.start()

    def start_pair(pair):
        start_down(pair[0])
        start_up(pair[1])

    def receive_pair(pair):
        @pl.when(me < n - 1)
        def _():
            for copy in pair[0]:
                copy.wait_recv()

        @pl.when(me > 0)
        def _():
            for copy in pair[1]:
                copy.wait_recv()

    def sent_pair(pair):
        @pl.when(me > 0)
        def _():
            for copy in pair[0]:
                copy.wait_send()

        @pl.when(me < n - 1)
        def _():
            for copy in pair[1]:
                copy.wait_send()

    def spread(step, send, recv, send_sem, recv_sem):
        copies = []
        for offset in sorted(range(1, n), key=lambda o: abs(2 * o - n)):
            target = lax.rem(me + offset, n)
            copies.append(
                pltpu.make_async_remote_copy(
                    src_ref=send.at[step, target],
                    dst_ref=recv.at[step, me],
                    send_sem=send_sem.at[step, offset],
                    recv_sem=recv_sem.at[step, offset],
                    device_id=peer(target),
                    device_id_type=MESH,
                )
            )
        return copies

    halve_rows = pairing((4 * rows, 4 * fine_rows), 1, 0.125)
    halve_cols = pairing((2 * LANES, LANES), 0, 1.0)
    double_rows = pairing((4 * fine_rows, 4 * rows), 0, 1.0)
    double_cols = pairing((LANES, 2 * LANES), 1, 1.0)

    def restrict_and_window(step):
        block = fields[step]
        parts = [block[f, 1, body, :] + block[f, 2, body, :] for f in range(3)]
        parts.append(
            jnp.exp(-thermal_gradient_factor * block[3, 1, body, :])
            + jnp.exp(-thermal_gradient_factor * block[3, 2, body, :])
        )
        short = times_left(halve_rows, jnp.concatenate(parts, 0))
        coarse = jnp.concatenate(
            [
                times_right(short[:, at : at + 2 * LANES], halve_cols)
                for at in range(0, width, 2 * LANES)
            ],
            1,
        )
        comps = [coarse[c * rows : (c + 1) * rows] for c in range(4)]
        comps[3] = comps[3] * zone_sigma[...]
        for target in range(n):
            first = target * xl - SWEEPS
            message = jnp.zeros((rows, LANES), jnp.float32)
            for c in range(4):
                moved = left_roll(comps[c], first - c * win)[:, :LANES]
                message = jnp.where(group == c, moved, message)
            send_f[step, target] = message

    def turned(value):
        return left_roll(value, win), left_roll(value, 2 * win), left_roll(value, 3 * win)

    def relax_all(step):
        x_at = me * xl - SWEEPS + inner
        valid = (x_at >= 0) & (x_at < cols) & (group < 3)

        def prepare(z):
            value = recv_f[step, z]
            one, two, three = turned(value)
            next_comp = jnp.where(group < 2, one, two)
            last_comp = jnp.where(group == 0, two, three)
            sigma = jnp.where(group == 0, three, jnp.where(group == 1, two, one))
            motional = next_comp * field2[z] - last_comp * field1[z]
            emf[z] = motional
            source[z] = sigma * motional + coil[z]
            inverse[z] = jnp.where(valid, 1.0 / (6.0 + coupling * sigma), 0.0)

        for z in range(depth):
            prepare(z)

        def sweep(old, new):
            for z in range(depth):
                centre = old[z + 1]
                total = source[z] + old[z] + old[z + 2]
                total = total + left_roll(centre, 1) + left_roll(centre, LANES - 1)
                total = total + jnp.where(sub == 0, 0.0, pltpu.roll(centre, 1, 0))
                total = total + jnp.where(sub == rows - 1, 0.0, pltpu.roll(centre, rows - 1, 0))
                new[z + 1] = total * inverse[z]

        def two_sweeps(index, carry):
            sweep(pot_a, pot_b)
            sweep(pot_b, pot_a)
            return carry

        lax.fori_loop(0, SWEEPS // 2, two_sweeps, 0)

        half = rows // 2
        packed = iota((half, LANES), 1) // xl

        def load(z):
            value = recv_f[step, z]
            one, two, three = turned(value)
            sigma = jnp.where(group == 0, three, jnp.where(group == 1, two, one))
            drive = emf[z] - coupling * pot_a[z + 1]
            current = sigma * drive + coil[z]
            one, two, three = turned(current)
            next_comp = jnp.where(group < 2, one, two)
            last_comp = jnp.where(group == 0, two, three)
            force = next_comp * field2[z] - last_comp * field1[z]
            one, two, three = turned(drive * drive)
            both = jnp.where(group == 3, value * (one + two + three), force)
            message = jnp.zeros((half, LANES), jnp.float32)
            for h in range(2):
                piece = both[h * half : (h + 1) * half]
                for c in range(4):
                    at = 4 * h + c
                    moved = left_roll(piece, c * win + SWEEPS - at * xl)
                    message = jnp.where(packed == at, moved, message)
            send_b[step, z] = message

        for z in range(depth):
            load(z)

    def prolong_loads(step):
        half = rows // 2
        packed = iota((half, LANES), 1) // xl
        per = LANES // xl
        strips = []
        for c in range(4):
            for h in range(2):
                strip = []
                for first in range(0, n, per):
                    piece = jnp.zeros((half, LANES), jnp.float32)
                    for d in range(per):
                        moved = left_roll(recv_b[step, first + d], (4 * h + c - d) * xl)
                        piece = jnp.where(packed == d, moved, piece)
                    strip.append(piece)
                strips.append(jnp.concatenate(strip, 1))
        coarse = jnp.concatenate(strips, 0)
        wide = jnp.concatenate(
            [
                times_right(coarse[:, at : at + LANES], double_cols)
                for at in range(0, cols, LANES)
            ],
            1,
        )
        loads[...] = times_left(double_rows, wide)

    def advance_all(step, store, done):
        block = fields[step]
        sub8 = iota((ROW, width), 0)
        lane8 = iota((ROW, width), 1)

        def chunk(plane, index):
            low = index * ROW
            at = low + ROW
            high = at + ROW
            here = pl.ds(at, ROW)
            centre = [block[f, plane, here, :] for f in range(6)]
            kinetic, dissip = centre[4], centre[5]
            eddy = eddy_coeff * kinetic * kinetic / jnp.maximum(dissip, turb_floor)
            diffuse = molecular + eddy
            strain = None
            for f in range(6):
                mid = centre[f]
                z_minus = block[f, plane - 1, here, :]
                z_plus = block[f, plane + 1, here, :]
                before = block[f, plane, pl.ds(low, ROW), :]
                after = block[f, plane, pl.ds(high, ROW), :]
                y_minus = pltpu.roll(jnp.where(sub8 == ROW - 1, before, mid), 1, 0)
                y_plus = pltpu.roll(jnp.where(sub8 == 0, after, mid), ROW - 1, 0)
                x_minus = jnp.where(lane8 == 0, 0.0, pltpu.roll(mid, 1, 1))
                x_plus = jnp.where(lane8 == width - 1, 0.0, pltpu.roll(mid, width - 1, 1))
                laplace = (
                    (z_plus + z_minus) + (y_plus + y_minus) + (x_plus + x_minus) - 6.0 * mid
                )
                grad_z = 0.5 * (z_plus - z_minus)
                grad_y = 0.5 * (y_plus - y_minus)
                grad_x = 0.5 * (x_plus - x_minus)
                transport = centre[0] * grad_x + centre[1] * grad_y + centre[2] * grad_z
                if f < 3:
                    square = grad_x * grad_x + grad_y * grad_y + grad_z * grad_z
                    strain = square if strain is None else strain + square
                if f < 4:
                    src = loads[pl.ds(f * fine_rows + index * ROW, ROW), :]
                elif f == 4:
                    produce = eddy * strain
                    src = produce - dissip
                else:
                    src = (
                        (prod_coeff * produce - dissip_coeff * dissip)
                        * dissip
                        / jnp.maximum(kinetic, turb_floor)
                    )
                if f == 3:
                    spread_by = heat_diffuse + eddy * (1.0 / 0.9)
                elif f == 5:
                    spread_by = molecular + eddy * (1.0 / 1.3)
                else:
                    spread_by = diffuse
                store(
                    f, plane, index, mid + time_step * (spread_by * laplace - transport + src)
                )

        for index in range(fine_rows // ROW):
            for plane in (1, 2):
                chunk(plane, index)
                done(plane, index)

    def store_mid(f, plane, index, value):
        fields1[f, plane, pl.ds(index * ROW + ROW, ROW), :] = value

    def store_last(f, plane, index, value):
        here = pl.ds(index * ROW, ROW)
        if f < 3:
            vel_out[f, plane - 1, here, :] = value
        elif f == 3:
            temp_out[plane - 1, here, :] = value
        else:
            turb_out[f - 4, plane - 1, here, :] = value

    def framed(own, arrived, index):
        tile, k = divmod(index, pack)
        left = left_roll(arrived[0, tile], SWEEPS * k)
        right = left_roll(arrived[1, tile], SWEEPS * k - (win - SWEEPS))
        whole = jnp.where(
            inner < SWEEPS, left, jnp.where(inner >= win - SWEEPS, right, own)
        )
        return jnp.where(group < 3, whole, 0.0)

    pl.semaphore_wait(barrier, n - 1)
    planes = first_faces(True), first_faces(False)
    halos = halo_copies(0)
    start_pair(halos)
    start_pair(planes)
    for fetch in fetches:
        fetch.wait()
    for row in (0, depth + 1):
        pot_a[row] = blank(LANES)
        pot_b[row] = blank(LANES)
    for step in range(STEPS):
        restrict_and_window(step)
        forward = spread(step, send_f, recv_f, f_send_sem, f_recv_sem)
        for copy in forward:
            copy.start()
        recv_f[step, me] = send_f[step, me]
        receive_pair(halos)
        if step == 0:
            for z in range(depth):
                pot_a[z + 1] = framed(own_ref[0, z], halo_in0, 3 * z)
                one, two, three = turned(framed(own_ref[1, z], halo_in0, 3 * z + 1))
                field1[z] = jnp.where(group < 2, one, two)
                field2[z] = jnp.where(group == 0, two, three)
                coil[z] = framed(own_ref[2, z], halo_in0, 3 * z + 2)
        else:
            for z in range(depth):
                pot_a[z + 1] = framed(pot_a[z + 1], halo_in1, z)
        for copy in forward:
            copy.wait_recv()
        relax_all(step)
        back = spread(step, send_b, recv_b, b_send_sem, b_recv_sem)
        for copy in back:
            copy.start()
        recv_b[step, me] = send_b[step, me]
        sent_pair(halos)
        if step == 0:
            pack_halos(
                halo_out1,
                [functools.partial(pot_a.__getitem__, z + 1) for z in range(depth)],
            )
            halos = halo_copies(1)
            start_pair(halos)
        else:
            for c in range(3):
                for z in range(depth):
                    at = c * win + SWEEPS
                    pot_out[c, z] = pot_a[z + 1][:, at : at + xl]
        for copy in forward:
            copy.wait_send()
        for copy in back:
            copy.wait_recv()
        prolong_loads(step)
        receive_pair(planes)
        if step == 0:
            following = later_faces(True), later_faces(False)

            def send_face(plane, index):
                if plane == 1:
                    start_down(following[0][index : index + 1])
                else:
                    start_up(following[1][index : index + 1])

            advance_all(step, store_mid, send_face)
        else:
            advance_all(step, store_last, lambda plane, index: None)
        for copy in back:
            copy.wait_send()
        sent_pair(planes)
        planes = following


def fused_on_device(
    melt_speeds,
    heat_state,
    eddy_quantities,
    zone_labels,
    zone_resistivity_inverse,
    imposed_induction,
    winding_current,
    window_entry_induction_guess,
):
    n = lax.axis_size("slab")
    _, xl, rows, depth = imposed_induction.shape
    _, fine_rows, width = heat_state.shape
    win = xl + 2 * SWEEPS
    coarse = [
        jnp.transpose(value, (0, 3, 2, 1))
        for value in (window_entry_induction_guess, imposed_induction, winding_current)
    ]

    def vmem(*shape):
        return pltpu.VMEM(shape, jnp.float32)

    plane = (depth, rows, LANES)
    dma = pltpu.SemaphoreType.DMA
    whole = pl.BlockSpec(memory_space=pltpu.VMEM)
    anywhere = pl.BlockSpec(memory_space=pl.ANY)
    vel, temp, turb, pot = pl.pallas_call(
        functools.partial(fused_kernel, n, xl),
        out_shape=(
            jax.ShapeDtypeStruct(melt_speeds.shape, jnp.float32),
            jax.ShapeDtypeStruct(heat_state.shape, jnp.float32),
            jax.ShapeDtypeStruct(eddy_quantities.shape, jnp.float32),
            jax.ShapeDtypeStruct((3, depth, rows, xl), jnp.float32),
        ),
        in_specs=[
            anywhere,
            anywhere,
            anywhere,
            whole,
            pl.BlockSpec(memory_space=pltpu.SMEM),
            whole,
            whole,
            whole,
        ],
        out_specs=(whole,) * 4,
        scratch_shapes=[
            vmem(6, 4, fine_rows + 2 * ROW, width),
            vmem(6, 4, fine_rows + 2 * ROW, width),
            vmem(STEPS, n, rows, LANES),
            vmem(STEPS, n, rows, LANES),
            vmem(STEPS, n, rows // 2, LANES),
            vmem(STEPS, n, rows // 2, LANES),
            vmem(3, *plane),
            vmem(2, 3 * depth * SWEEPS // win, rows, LANES),
            vmem(2, 3 * depth * SWEEPS // win, rows, LANES),
            vmem(2, depth * SWEEPS // win, rows, LANES),
            vmem(2, depth * SWEEPS // win, rows, LANES),
            vmem(depth + 2, rows, LANES),
            vmem(depth + 2, rows, LANES),
            vmem(*plane),
            vmem(*plane),
            vmem(*plane),
            vmem(*plane),
            vmem(*plane),
            vmem(*plane),
            vmem(4 * fine_rows, width),
            vmem(rows, width // 2),
            dma((3,)),
            dma((STEPS, n)),
            dma((STEPS, n)),
            dma((STEPS, n)),
            dma((STEPS, n)),
            dma((STEPS, 2, max(3, fine_rows // ROW))),
            dma((STEPS, 2, max(3, fine_rows // ROW))),
            dma((STEPS, 2)),
            dma((STEPS, 2)),
        ],
        compiler_params=pltpu.CompilerParams(
            collective_id=0, has_side_effects=True, vmem_limit_bytes=40 * 1024 * 1024
        ),
    )(melt_speeds, heat_state, eddy_quantities, zone_labels, zone_resistivity_inverse, *coarse)
    return vel, temp, turb, jnp.transpose(pot, (0, 3, 2, 1))


def fits_fused(n, heat_state, imposed_induction):
    _, xl, rows, depth = imposed_induction.shape
    planes, fine_rows, width = heat_state.shape
    win = xl + 2 * SWEEPS
    return (
        STEPS == 2
        and SWEEPS % 2 == 0
        and n > 1
        and planes == 2
        and depth == n
        and rows == 2 * ROW
        and fine_rows == 2 * rows
        and width == 2 * n * xl
        and width % (4 * LANES) == 0
        and 4 * win == LANES
        and xl == 2 * SWEEPS
        and n % (LANES // xl) == 0
        and depth % (win // SWEEPS) == 0
    )


def on_device(*args):
    if fits_fused(lax.axis_size("slab"), args[1], args[5]):
        return fused_on_device(*args)
    return layered_on_device(*args)


def solution(mesh):
    return jax.shard_map(
        on_device,
        mesh=mesh,
        in_specs=(
            P(None, ("groups", "slab"), None, None),
            P(("groups", "slab"), None, None),
            P(None, ("groups", "slab"), None, None),
            P(("groups", "slab"), None, None),
            P(),
            P(None, ("groups", "slab"), None, None),
            P(None, ("groups", "slab"), None, None),
            P(None, ("groups", "slab"), None, None),
        ),
        out_specs=(
            P(None, ("groups", "slab"), None, None),
            P(("groups", "slab"), None, None),
            P(None, ("groups", "slab"), None, None),
            P(None, ("groups", "slab"), None, None),
        ),
        check_vma=False,
    )
```

```python
import functools

import jax
import jax.numpy as jnp
from jax import lax
from jax.experimental import pallas as pl
from jax.experimental.pallas import tpu as pltpu
from jax.sharding import PartitionSpec as P

STEPS = 2
SWEEPS = 8


time_step = 0.02
molecular = 0.01
heat_diffuse = 0.01
eddy_coeff = 0.09
prod_coeff = 1.44
dissip_coeff = 1.92
turb_floor = 0.05
coupling = 1.0
thermal_gradient_factor = 0.3


def extended(block, sides, width):
    for axis, dim in sides:
        count = lax.axis_size(axis)
        forward = [(i, i + 1) for i in range(count - 1)]
        backward = [(target, source) for source, target in forward]
        low = lax.ppermute(
            lax.slice_in_dim(block, block.shape[dim] - width, None, axis=dim), axis, forward
        )
        high = lax.ppermute(lax.slice_in_dim(block, 0, width, axis=dim), axis, backward)
        block = jnp.concatenate([low, block, high], axis=dim)
    return block


def reduce_onto_parent(block):
    comps, depth, rows, cols = block.shape
    shaped = block.reshape(comps, depth // 2, 2, rows // 2, 2, cols // 2, 2)
    return jnp.mean(shaped, axis=(2, 4, 6))


def prolong(block):
    comps, depth, rows, cols = block.shape
    wide = jnp.broadcast_to(
        block[:, :, None, :, None, :, None], (comps, depth, 2, rows, 2, cols, 2)
    )
    return wide.reshape(comps, depth * 2, rows * 2, cols * 2)


def cross(left_vec, right_vec):
    return jnp.stack(
        [
            left_vec[1] * right_vec[2] - left_vec[2] * right_vec[1],
            left_vec[2] * right_vec[0] - left_vec[0] * right_vec[2],
            left_vec[0] * right_vec[1] - left_vec[1] * right_vec[0],
        ],
        0,
    )


def neighbours(padded):
    return (
        padded[:, 2:, 1:-1, 1:-1]
        + padded[:, :-2, 1:-1, 1:-1]
        + padded[:, 1:-1, 2:, 1:-1]
        + padded[:, 1:-1, :-2, 1:-1]
        + padded[:, 1:-1, 1:-1, 2:]
        + padded[:, 1:-1, 1:-1, :-2]
    )


def ohmic_admittance(zone_labels, zone_resistivity_inverse, heat_state):
    labels = jnp.arange(zone_resistivity_inverse.shape[0], dtype=jnp.int32)
    onehot = zone_labels[None] == labels[:, None, None, None]
    searched_higher = jnp.sum(
        jnp.where(onehot, zone_resistivity_inverse[:, None, None, None], jnp.float32(0.0)), axis=0
    )
    return (
        searched_higher
        * reduce_onto_parent(jnp.exp(-thermal_gradient_factor * heat_state)[None])[0]
    )


def faces(potential):
    padded = extended(potential, (("slab", 1),), 1)
    return jnp.pad(padded, ((0, 0), (0, 0), (1, 1), (1, 1)))


def relax(coupled, imposed_induction, winding_current, potential):
    conduct = coupled[3]
    motional = cross(coupled[:3], imposed_induction)
    source = conduct * motional + winding_current
    diagonal = 6.0 + coupling * conduct
    for sweep_index in range(SWEEPS):
        potential = (source + neighbours(faces(potential))) / diagonal
    drive_field = motional - coupling * potential
    current = conduct * drive_field + winding_current
    lorentz = cross(current, imposed_induction)
    joule = conduct * jnp.sum(drive_field * drive_field, axis=0)
    return (potential, jnp.concatenate([lorentz, joule[None]], 0))


def advance(padded, lorentz, joule):
    bordered = jnp.pad(padded, ((0, 0), (0, 0), (0, 0), (1, 1)))
    center = bordered[:, 1:-1, 1:-1, 1:-1]
    z_plus = bordered[:, 2:, 1:-1, 1:-1]
    z_minus = bordered[:, :-2, 1:-1, 1:-1]
    y_plus = bordered[:, 1:-1, 2:, 1:-1]
    y_minus = bordered[:, 1:-1, :-2, 1:-1]
    x_plus = bordered[:, 1:-1, 1:-1, 2:]
    x_minus = bordered[:, 1:-1, 1:-1, :-2]
    grad_z = 0.5 * (z_plus - z_minus)
    grad_y = 0.5 * (y_plus - y_minus)
    grad_x = 0.5 * (x_plus - x_minus)
    laplace = z_plus + z_minus + y_plus + y_minus + x_plus + x_minus - 6.0 * center
    kinetic = center[4]
    dissip = center[5]
    transport = center[0] * grad_x + center[1] * grad_y + center[2] * grad_z
    eddy_visc = eddy_coeff * kinetic * kinetic / jnp.maximum(dissip, turb_floor)
    strain = jnp.sum(
        grad_x[:3] * grad_x[:3] + grad_y[:3] * grad_y[:3] + grad_z[:3] * grad_z[:3], axis=0
    )
    produce = eddy_visc * strain
    diffuse = jnp.stack(
        [
            molecular + eddy_visc,
            molecular + eddy_visc,
            molecular + eddy_visc,
            heat_diffuse + eddy_visc / 0.9,
            molecular + eddy_visc,
            molecular + eddy_visc / 1.3,
        ],
        0,
    )
    dissip_source = (
        (prod_coeff * produce - dissip_coeff * dissip) * dissip / jnp.maximum(kinetic, turb_floor)
    )
    source = jnp.concatenate(
        [lorentz, joule[None], (produce - dissip)[None], dissip_source[None]], 0
    )
    return center + time_step * (diffuse * laplace - transport + source)


def flow_step(induction_tables, em_loads):
    padded = extended(induction_tables, (("slab", 1),), 1)
    padded = jnp.pad(padded, ((0, 0), (0, 0), (1, 1), (0, 0)))
    return advance(padded, em_loads[:3], em_loads[3])


def local_coupled(induction_tables, zone_labels, zone_resistivity_inverse):
    conduct = ohmic_admittance(zone_labels, zone_resistivity_inverse, induction_tables[3])
    return jnp.concatenate([reduce_onto_parent(induction_tables[:3]), conduct[None]], 0)


def layered_on_device(
    melt_speeds,
    heat_state,
    eddy_quantities,
    zone_labels,
    zone_resistivity_inverse,
    imposed_induction,
    winding_current,
    window_entry_induction_guess,
):
    induction_tables = jnp.concatenate([melt_speeds, heat_state[None], eddy_quantities], 0)
    arrived = (
        lax.all_to_all(
            window_entry_induction_guess, "slab", split_axis=3, concat_axis=1, tiled=True
        ),
        lax.all_to_all(imposed_induction, "slab", split_axis=3, concat_axis=1, tiled=True),
        lax.all_to_all(winding_current, "slab", split_axis=3, concat_axis=1, tiled=True),
    )
    potential = jnp.transpose(arrived[0], (0, 3, 2, 1))
    field_local = jnp.transpose(arrived[1], (0, 3, 2, 1))
    coil_local = jnp.transpose(arrived[2], (0, 3, 2, 1))
    for step_index in range(STEPS):
        coupled = local_coupled(induction_tables, zone_labels, zone_resistivity_inverse)
        potential, em_loads = relax(coupled, field_local, coil_local, potential)
        induction_tables = flow_step(induction_tables, prolong(em_loads))
    potential = lax.all_to_all(
        jnp.transpose(potential, (0, 3, 2, 1)), "slab", split_axis=1, concat_axis=3, tiled=True
    )
    return (induction_tables[:3], induction_tables[3], induction_tables[4:], potential)


ROW = 8
LANES = 128
MESH = pl.DeviceIdType.MESH


def iota(shape, dim):
    return lax.broadcasted_iota(jnp.int32, shape, dim)


def thirds(value):
    high = value.astype(jnp.bfloat16)
    rest = value - high.astype(jnp.float32)
    middle = rest.astype(jnp.bfloat16)
    low = (rest - middle.astype(jnp.float32)).astype(jnp.bfloat16)
    return high, middle, low


def times_right(value, matrix):
    rows = value.shape[0]
    out = jnp.dot(
        jnp.concatenate(thirds(value), 0), matrix, preferred_element_type=jnp.float32
    )
    return out[:rows] + out[rows : 2 * rows] + out[2 * rows :]


def times_left(matrix, value):
    return jnp.dot(
        jnp.concatenate([matrix] * 3, 1),
        jnp.concatenate(thirds(value), 0),
        preferred_element_type=jnp.float32,
    )


def pairing(shape, fine_dim, scale):
    fine = lax.shift_right_logical(iota(shape, fine_dim), 1)
    return jnp.where(fine == iota(shape, 1 - fine_dim), scale, 0.0).astype(jnp.bfloat16)


def left_roll(value, shift):
    width = value.shape[-1]
    shift = shift % width
    return value if shift == 0 else pltpu.roll(value, width - shift, value.ndim - 1)


def fused_kernel(
    n,
    xl,
    melt_ref,
    heat_ref,
    eddy_ref,
    zone_ref,
    table_ref,
    guess_ref,
    induction_ref,
    winding_ref,
    vel_out,
    temp_out,
    turb_out,
    pot_out,
    fields0,
    fields1,
    send_f,
    recv_f,
    send_b,
    recv_b,
    own_ref,
    halo_out0,
    halo_in0,
    halo_out1,
    halo_in1,
    pot_a,
    pot_b,
    field1,
    field2,
    coil,
    emf,
    source,
    inverse,
    loads,
    zone_sigma,
    load_sem,
    f_send_sem,
    f_recv_sem,
    b_send_sem,
    b_recv_sem,
    p_send_sem,
    p_recv_sem,
    h_send_sem,
    h_recv_sem,
):
    me = lax.axis_index("slab")
    fields = (fields0, fields1)
    halo_out = (halo_out0, halo_out1)
    halo_in = (halo_in0, halo_in1)
    win = xl + 2 * SWEEPS
    depth, rows = guess_ref.shape[1:3]
    fine_rows, width = heat_ref.shape[1:]
    body = pl.ds(ROW, fine_rows)
    cols = width // 2
    lane = iota((rows, LANES), 1)
    group = lane // win
    inner = lane % win
    sub = iota((rows, LANES), 0)

    def peer(index):
        return {"slab": index}

    fetches = [
        pltpu.make_async_copy(melt_ref, fields0.at[0:3, 1:3, body, :], load_sem.at[0]),
        pltpu.make_async_copy(heat_ref, fields0.at[3, 1:3, body, :], load_sem.at[1]),
        pltpu.make_async_copy(eddy_ref, fields0.at[4:6, 1:3, body, :], load_sem.at[2]),
    ]
    for fetch in fetches:
        fetch.start()

    barrier = pltpu.get_barrier_semaphore()
    for offset in range(1, n):
        pl.semaphore_signal(
            barrier, inc=1, device_id=peer(lax.rem(me + offset, n)), device_id_type=MESH
        )

    for block in fields:
        edge = jnp.zeros((6, 4, ROW, width), jnp.float32)
        block[:, :, 0:ROW, :] = edge
        block[:, :, ROW + fine_rows :, :] = edge

    @pl.when(me == 0)
    def _():
        for block in fields:
            block[:, 0, body, :] = jnp.zeros((6, fine_rows, width), jnp.float32)
        for block in halo_in:
            block[0] = jnp.zeros(block.shape[1:], jnp.float32)

    @pl.when(me == n - 1)
    def _():
        for block in fields:
            block[:, 3, body, :] = jnp.zeros((6, fine_rows, width), jnp.float32)
        for block in halo_in:
            block[1] = jnp.zeros(block.shape[1:], jnp.float32)

    labels = zone_ref[0]
    sigma0 = jnp.zeros(labels.shape, jnp.float32)
    for region in range(table_ref.shape[0]):
        sigma0 = sigma0 + jnp.where(labels == region, table_ref[region], 0.0)
    zone_sigma[...] = sigma0

    def blank(lanes):
        return jnp.zeros((rows, lanes), jnp.float32)

    for a, coarse_ref in enumerate((guess_ref, induction_ref, winding_ref)):
        for z in range(depth):
            own_ref[a, z] = jnp.concatenate(
                [
                    blank(SWEEPS),
                    coarse_ref[0, z],
                    blank(2 * SWEEPS),
                    coarse_ref[1, z],
                    blank(2 * SWEEPS),
                    coarse_ref[2, z],
                    blank(SWEEPS + win),
                ],
                1,
            )

    slot = inner // SWEEPS
    pack = win // SWEEPS

    def pack_halos(out, values):
        for first in range(0, len(values), pack):
            to_left = blank(LANES)
            to_right = blank(LANES)
            for k in range(pack):
                value = values[first + k]()
                to_left = jnp.where(slot == k, left_roll(value, SWEEPS - SWEEPS * k), to_left)
                to_right = jnp.where(slot == k, left_roll(value, xl - SWEEPS * k), to_right)
            out[0, first // pack] = to_left
            out[1, first // pack] = to_right

    pack_halos(
        halo_out0,
        [functools.partial(own_ref.__getitem__, (a, z)) for z in range(depth) for a in range(3)],
    )

    pieces = fine_rows // ROW

    def face_copies(step, down):
        side = 0 if down else 1
        copies = []
        for part in range(pieces):
            here = pl.ds(ROW + part * ROW, ROW)
            copies.append(
                pltpu.make_async_remote_copy(
                    src_ref=fields[step].at[:, 1 + side, here, :],
                    dst_ref=fields[step].at[:, 3 - 3 * side, here, :],
                    send_sem=p_send_sem.at[step, side, part],
                    recv_sem=p_recv_sem.at[step, side, part],
                    device_id=peer(me - 1 if down else me + 1),
                    device_id_type=MESH,
                )
            )
        return copies

    def halo_copies(step):
        down = pltpu.make_async_remote_copy(
            src_ref=halo_out[step].at[0],
            dst_ref=halo_in[step].at[1],
            send_sem=h_send_sem.at[step, 0],
            recv_sem=h_recv_sem.at[step, 0],
            device_id=peer(me - 1),
            device_id_type=MESH,
        )
        up = pltpu.make_async_remote_copy(
            src_ref=halo_out[step].at[1],
            dst_ref=halo_in[step].at[0],
            send_sem=h_send_sem.at[step, 1],
            recv_sem=h_recv_sem.at[step, 1],
            device_id=peer(me + 1),
            device_id_type=MESH,
        )
        return [down], [up]

    def start_down(copies):
        @pl.when(me > 0)
        def _():
            for copy in copies:
                copy.start()

    def start_up(copies):
        @pl.when(me < n - 1)
        def _():
            for copy in copies:
                copy.start()

    def start_pair(pair):
        start_down(pair[0])
        start_up(pair[1])

    def receive_pair(pair):
        if pair[0]:

            @pl.when(me < n - 1)
            def _():
                for copy in pair[0]:
                    copy.wait_recv()

        if pair[1]:

            @pl.when(me > 0)
            def _():
                for copy in pair[1]:
                    copy.wait_recv()

    def sent_pair(pair):
        @pl.when(me > 0)
        def _():
            for copy in pair[0]:
                copy.wait_send()

        @pl.when(me < n - 1)
        def _():
            for copy in pair[1]:
                copy.wait_send()

    def spread(step, send, recv, send_sem, recv_sem):
        copies = []
        for offset in sorted(range(1, n), key=lambda o: abs(2 * o - n)):
            target = lax.rem(me + offset, n)
            copies.append(
                pltpu.make_async_remote_copy(
                    src_ref=send.at[step, target],
                    dst_ref=recv.at[step, me],
                    send_sem=send_sem.at[step, offset],
                    recv_sem=recv_sem.at[step, offset],
                    device_id=peer(target),
                    device_id_type=MESH,
                )
            )
        return copies

    halve_rows = pairing((4 * rows, 4 * fine_rows), 1, 0.125)
    halve_cols = pairing((2 * LANES, LANES), 0, 1.0)
    double_rows = pairing((4 * fine_rows, 4 * rows), 0, 1.0)
    double_cols = pairing((LANES, 2 * LANES), 1, 1.0)

    def restrict_and_window(step):
        block = fields[step]
        parts = [block[f, 1, body, :] + block[f, 2, body, :] for f in range(3)]
        parts.append(
            jnp.exp(-thermal_gradient_factor * block[3, 1, body, :])
            + jnp.exp(-thermal_gradient_factor * block[3, 2, body, :])
        )
        short = times_left(halve_rows, jnp.concatenate(parts, 0))
        coarse = jnp.concatenate(
            [
                times_right(short[:, at : at + 2 * LANES], halve_cols)
                for at in range(0, width, 2 * LANES)
            ],
            1,
        )
        comps = [coarse[c * rows : (c + 1) * rows] for c in range(4)]
        comps[3] = comps[3] * zone_sigma[...]
        for target in range(n):
            first = target * xl - SWEEPS
            message = jnp.zeros((rows, LANES), jnp.float32)
            for c in range(4):
                moved = left_roll(comps[c], first - c * win)[:, :LANES]
                message = jnp.where(group == c, moved, message)
            send_f[step, target] = message

    def turned(value):
        return left_roll(value, win), left_roll(value, 2 * win), left_roll(value, 3 * win)

    def relax_all(step):
        x_at = me * xl - SWEEPS + inner
        valid = (x_at >= 0) & (x_at < cols) & (group < 3)

        def prepare(z):
            value = recv_f[step, z]
            one, two, three = turned(value)
            next_comp = jnp.where(group < 2, one, two)
            last_comp = jnp.where(group == 0, two, three)
            sigma = jnp.where(group == 0, three, jnp.where(group == 1, two, one))
            motional = next_comp * field2[z] - last_comp * field1[z]
            emf[z] = motional
            source[z] = sigma * motional + coil[z]
            inverse[z] = jnp.where(valid, 1.0 / (6.0 + coupling * sigma), 0.0)

        for z in range(depth):
            prepare(z)

        def sweep(old, new):
            for z in range(depth):
                centre = old[z + 1]
                total = source[z] + old[z] + old[z + 2]
                total = total + left_roll(centre, 1) + left_roll(centre, LANES - 1)
                total = total + jnp.where(sub == 0, 0.0, pltpu.roll(centre, 1, 0))
                total = total + jnp.where(sub == rows - 1, 0.0, pltpu.roll(centre, rows - 1, 0))
                new[z + 1] = total * inverse[z]

        def two_sweeps(index, carry):
            sweep(pot_a, pot_b)
            sweep(pot_b, pot_a)
            return carry

        lax.fori_loop(0, SWEEPS // 2, two_sweeps, 0)

        half = rows // 2
        packed = iota((half, LANES), 1) // xl

        def load(z):
            value = recv_f[step, z]
            one, two, three = turned(value)
            sigma = jnp.where(group == 0, three, jnp.where(group == 1, two, one))
            drive = emf[z] - coupling * pot_a[z + 1]
            current = sigma * drive + coil[z]
            one, two, three = turned(current)
            next_comp = jnp.where(group < 2, one, two)
            last_comp = jnp.where(group == 0, two, three)
            force = next_comp * field2[z] - last_comp * field1[z]
            one, two, three = turned(drive * drive)
            both = jnp.where(group == 3, value * (one + two + three), force)
            message = jnp.zeros((half, LANES), jnp.float32)
            for h in range(2):
                piece = both[h * half : (h + 1) * half]
                for c in range(4):
                    at = 4 * h + c
                    moved = left_roll(piece, c * win + SWEEPS - at * xl)
                    message = jnp.where(packed == at, moved, message)
            send_b[step, z] = message

        for z in range(depth):
            load(z)

    def prolong_loads(step):
        half = rows // 2
        packed = iota((half, LANES), 1) // xl
        per = LANES // xl
        strips = []
        for c in range(4):
            for h in range(2):
                strip = []
                for first in range(0, n, per):
                    piece = jnp.zeros((half, LANES), jnp.float32)
                    for d in range(per):
                        moved = left_roll(recv_b[step, first + d], (4 * h + c - d) * xl)
                        piece = jnp.where(packed == d, moved, piece)
                    strip.append(piece)
                strips.append(jnp.concatenate(strip, 1))
        coarse = jnp.concatenate(strips, 0)
        wide = jnp.concatenate(
            [
                times_right(coarse[:, at : at + LANES], double_cols)
                for at in range(0, cols, LANES)
            ],
            1,
        )
        loads[...] = times_left(double_rows, wide)

    def advance_all(step, store, ready, done):
        block = fields[step]
        sub8 = iota((ROW, width), 0)
        lane8 = iota((ROW, width), 1)

        def chunk(plane, index):
            low = index * ROW
            at = low + ROW
            high = at + ROW
            here = pl.ds(at, ROW)
            centre = [block[f, plane, here, :] for f in range(6)]
            kinetic, dissip = centre[4], centre[5]
            eddy = eddy_coeff * kinetic * kinetic / jnp.maximum(dissip, turb_floor)
            diffuse = molecular + eddy
            strain = None
            for f in range(6):
                mid = centre[f]
                z_minus = block[f, plane - 1, here, :]
                z_plus = block[f, plane + 1, here, :]
                before = block[f, plane, pl.ds(low, ROW), :]
                after = block[f, plane, pl.ds(high, ROW), :]
                y_minus = pltpu.roll(jnp.where(sub8 == ROW - 1, before, mid), 1, 0)
                y_plus = pltpu.roll(jnp.where(sub8 == 0, after, mid), ROW - 1, 0)
                x_minus = jnp.where(lane8 == 0, 0.0, pltpu.roll(mid, 1, 1))
                x_plus = jnp.where(lane8 == width - 1, 0.0, pltpu.roll(mid, width - 1, 1))
                laplace = (
                    (z_plus + z_minus) + (y_plus + y_minus) + (x_plus + x_minus) - 6.0 * mid
                )
                grad_z = 0.5 * (z_plus - z_minus)
                grad_y = 0.5 * (y_plus - y_minus)
                grad_x = 0.5 * (x_plus - x_minus)
                transport = centre[0] * grad_x + centre[1] * grad_y + centre[2] * grad_z
                if f < 3:
                    square = grad_x * grad_x + grad_y * grad_y + grad_z * grad_z
                    strain = square if strain is None else strain + square
                if f < 4:
                    src = loads[pl.ds(f * fine_rows + index * ROW, ROW), :]
                elif f == 4:
                    produce = eddy * strain
                    src = produce - dissip
                else:
                    src = (
                        (prod_coeff * produce - dissip_coeff * dissip)
                        * dissip
                        / jnp.maximum(kinetic, turb_floor)
                    )
                if f == 3:
                    spread_by = heat_diffuse + eddy * (1.0 / 0.9)
                elif f == 5:
                    spread_by = molecular + eddy * (1.0 / 1.3)
                else:
                    spread_by = diffuse
                store(
                    f, plane, index, mid + time_step * (spread_by * laplace - transport + src)
                )

        for index in range(fine_rows // ROW):
            for plane in (1, 2):
                ready(plane, index)
                chunk(plane, index)
                done(plane, index)

    def store_mid(f, plane, index, value):
        fields1[f, plane, pl.ds(index * ROW + ROW, ROW), :] = value

    def store_last(f, plane, index, value):
        here = pl.ds(index * ROW, ROW)
        if f < 3:
            vel_out[f, plane - 1, here, :] = value
        elif f == 3:
            temp_out[plane - 1, here, :] = value
        else:
            turb_out[f - 4, plane - 1, here, :] = value

    def framed(own, arrived, index):
        tile, k = divmod(index, pack)
        left = left_roll(arrived[0, tile], SWEEPS * k)
        right = left_roll(arrived[1, tile], SWEEPS * k - (win - SWEEPS))
        whole = jnp.where(
            inner < SWEEPS, left, jnp.where(inner >= win - SWEEPS, right, own)
        )
        return jnp.where(group < 3, whole, 0.0)

    pl.semaphore_wait(barrier, n - 1)
    planes = face_copies(0, True), face_copies(0, False)
    halos = halo_copies(0)
    start_pair(halos)
    for fetch in fetches:
        fetch.wait()
    for row in (0, depth + 1):
        pot_a[row] = blank(LANES)
        pot_b[row] = blank(LANES)
    for step in range(STEPS):
        restrict_and_window(step)
        forward = spread(step, send_f, recv_f, f_send_sem, f_recv_sem)
        for copy in forward:
            copy.start()
        if step == 0:
            start_pair([side[: pieces // 2] for side in planes])
        else:
            start_pair([side[pieces // 2 :] for side in planes])
        recv_f[step, me] = send_f[step, me]
        receive_pair(halos)
        if step == 0:
            for z in range(depth):
                pot_a[z + 1] = framed(own_ref[0, z], halo_in0, 3 * z)
                one, two, three = turned(framed(own_ref[1, z], halo_in0, 3 * z + 1))
                field1[z] = jnp.where(group < 2, one, two)
                field2[z] = jnp.where(group == 0, two, three)
                coil[z] = framed(own_ref[2, z], halo_in0, 3 * z + 2)
        else:
            for z in range(depth):
                pot_a[z + 1] = framed(pot_a[z + 1], halo_in1, z)
        for copy in forward:
            copy.wait_recv()
        relax_all(step)
        back = spread(step, send_b, recv_b, b_send_sem, b_recv_sem)
        for copy in back:
            copy.start()
        recv_b[step, me] = send_b[step, me]
        sent_pair(halos)
        if step == 0:
            start_pair([side[pieces // 2 :] for side in planes])
            pack_halos(
                halo_out1,
                [functools.partial(pot_a.__getitem__, z + 1) for z in range(depth)],
            )
            halos = halo_copies(1)
            start_pair(halos)
        else:
            for c in range(3):
                for z in range(depth):
                    at = c * win + SWEEPS
                    pot_out[c, z] = pot_a[z + 1][:, at : at + xl]
        for copy in forward:
            copy.wait_send()
        for copy in back:
            copy.wait_recv()
        prolong_loads(step)
        if step == 0:
            following = face_copies(1, True), face_copies(1, False)

        def ready(plane, index):
            if plane == 1:
                receive_pair([[], planes[1][index : index + 1]])
            else:
                receive_pair([planes[0][index : index + 1], []])

        def done(plane, index):
            if step > 0 or index >= pieces // 2:
                return
            if plane == 1:
                start_down(following[0][index : index + 1])
            else:
                start_up(following[1][index : index + 1])

        advance_all(step, store_mid if step == 0 else store_last, ready, done)
        for copy in back:
            copy.wait_send()
        sent_pair(planes)
        planes = following


def fused_on_device(
    melt_speeds,
    heat_state,
    eddy_quantities,
    zone_labels,
    zone_resistivity_inverse,
    imposed_induction,
    winding_current,
    window_entry_induction_guess,
):
    n = lax.axis_size("slab")
    _, xl, rows, depth = imposed_induction.shape
    _, fine_rows, width = heat_state.shape
    win = xl + 2 * SWEEPS
    coarse = [
        jnp.transpose(value, (0, 3, 2, 1))
        for value in (window_entry_induction_guess, imposed_induction, winding_current)
    ]

    def vmem(*shape):
        return pltpu.VMEM(shape, jnp.float32)

    plane = (depth, rows, LANES)
    dma = pltpu.SemaphoreType.DMA
    whole = pl.BlockSpec(memory_space=pltpu.VMEM)
    anywhere = pl.BlockSpec(memory_space=pl.ANY)
    vel, temp, turb, pot = pl.pallas_call(
        functools.partial(fused_kernel, n, xl),
        out_shape=(
            jax.ShapeDtypeStruct(melt_speeds.shape, jnp.float32),
            jax.ShapeDtypeStruct(heat_state.shape, jnp.float32),
            jax.ShapeDtypeStruct(eddy_quantities.shape, jnp.float32),
            jax.ShapeDtypeStruct((3, depth, rows, xl), jnp.float32),
        ),
        in_specs=[
            anywhere,
            anywhere,
            anywhere,
            whole,
            pl.BlockSpec(memory_space=pltpu.SMEM),
            whole,
            whole,
            whole,
        ],
        out_specs=(whole,) * 4,
        scratch_shapes=[
            vmem(6, 4, fine_rows + 2 * ROW, width),
            vmem(6, 4, fine_rows + 2 * ROW, width),
            vmem(STEPS, n, rows, LANES),
            vmem(STEPS, n, rows, LANES),
            vmem(STEPS, n, rows // 2, LANES),
            vmem(STEPS, n, rows // 2, LANES),
            vmem(3, *plane),
            vmem(2, 3 * depth * SWEEPS // win, rows, LANES),
            vmem(2, 3 * depth * SWEEPS // win, rows, LANES),
            vmem(2, depth * SWEEPS // win, rows, LANES),
            vmem(2, depth * SWEEPS // win, rows, LANES),
            vmem(depth + 2, rows, LANES),
            vmem(depth + 2, rows, LANES),
            vmem(*plane),
            vmem(*plane),
            vmem(*plane),
            vmem(*plane),
            vmem(*plane),
            vmem(*plane),
            vmem(4 * fine_rows, width),
            vmem(rows, width // 2),
            dma((3,)),
            dma((STEPS, n)),
            dma((STEPS, n)),
            dma((STEPS, n)),
            dma((STEPS, n)),
            dma((STEPS, 2, fine_rows // ROW)),
            dma((STEPS, 2, fine_rows // ROW)),
            dma((STEPS, 2)),
            dma((STEPS, 2)),
        ],
        compiler_params=pltpu.CompilerParams(
            collective_id=0, has_side_effects=True, vmem_limit_bytes=40 * 1024 * 1024
        ),
    )(melt_speeds, heat_state, eddy_quantities, zone_labels, zone_resistivity_inverse, *coarse)
    return vel, temp, turb, jnp.transpose(pot, (0, 3, 2, 1))


def fits_fused(n, heat_state, imposed_induction):
    _, xl, rows, depth = imposed_induction.shape
    planes, fine_rows, width = heat_state.shape
    win = xl + 2 * SWEEPS
    return (
        STEPS == 2
        and SWEEPS % 2 == 0
        and n > 1
        and planes == 2
        and depth == n
        and rows == 2 * ROW
        and fine_rows == 2 * rows
        and width == 2 * n * xl
        and width % (4 * LANES) == 0
        and 4 * win == LANES
        and xl == 2 * SWEEPS
        and n % (LANES // xl) == 0
        and depth % (win // SWEEPS) == 0
    )


def on_device(*args):
    if fits_fused(lax.axis_size("slab"), args[1], args[5]):
        return fused_on_device(*args)
    return layered_on_device(*args)


def solution(mesh):
    return jax.shard_map(
        on_device,
        mesh=mesh,
        in_specs=(
            P(None, ("groups", "slab"), None, None),
            P(("groups", "slab"), None, None),
            P(None, ("groups", "slab"), None, None),
            P(("groups", "slab"), None, None),
            P(),
            P(None, ("groups", "slab"), None, None),
            P(None, ("groups", "slab"), None, None),
            P(None, ("groups", "slab"), None, None),
        ),
        out_specs=(
            P(None, ("groups", "slab"), None, None),
            P(("groups", "slab"), None, None),
            P(None, ("groups", "slab"), None, None),
            P(None, ("groups", "slab"), None, None),
        ),
        check_vma=False,
    )
```
